128 devices in a mesh: beam: 64 (over z_lo, y, x, core), row: 2 (over z_hi).
Axes of the slice: x: 4, y: 4, z: 4 (z_hi: 2, z_lo: 2; z = z_hi * 2 + z_lo), core: 2. Of those that a mesh axis runs over, the one named last changes fastest.
Arguments:
- tilts: int32 [128, 2], P('beam'), may hold values from -64 to 64
- potentials: bfloat16 [64, 1024, 1024], P('beam', 'row'), may hold values from 0 to 2
- owners: int32 [2], replicated, may hold values from 0 to 63
- beam_amplitude: float32 [128], P('beam'), may hold values from 0.5 to 1.5
- beam_phase: float32 [128], P('beam'), may hold values from -3.140625 to 3.140625
- probe_positions: int32 [128, 2], replicated, may hold values from 0 to 1023, as said below
- beam_offsets: int32 [128], replicated, may hold values from 0 to 127
Outputs:
- exit_waves: bfloat16 [128, 1024, 2048], P('beam', 'row')
- probe_waves: float32 [2, 64, 64, 128], P('row', 'beam')
The draws below stay inside these ranges and needn't reach their ends.
Inputs may be any that keep to these rules, and one draw needn't show every extreme that they name: `probe_positions`: probe p's row coordinate Y_p lies in rows (p // 64) * 512 to (p // 64 + 1) * 512 - 1; its column coordinate is any pixel.
All inputs are finite; a program needn't handle non-finite values.
Results may differ from the reference program's by a relative error of at most 0.0073.
Values may be sent and summed in bfloat16 or wider, within the bound.
A program may use at most 128 MiB of HBM per device.

```python
import math
import jax
import jax.numpy as jnp
import numpy as np
from jax import lax

NPIX = 1024
SLICES = 2
RAD = 8
WIN = 64
BEAMS = 128
ROWS_DEV = 512
PROBE_BLOCK = 64
PROBES = 128
TILES = 64
N_ROW = 2


def draw_probe_positions(key, part):
    first_key = jax.random.fold_in(key, 11)
    second_key = jax.random.fold_in(key, 23)
    block_ids = jnp.arange(PROBES, dtype=jnp.int32) // PROBE_BLOCK
    row_coord = block_ids * ROWS_DEV + jax.random.randint(first_key, (PROBES,), 0, ROWS_DEV, dtype=jnp.int32)
    column_coord = jax.random.randint(second_key, (PROBES,), 0, NPIX, dtype=jnp.int32)
    row_coord = row_coord.at[0].set(0).at[PROBES - 1].set(NPIX - 1)
    column_coord = column_coord.at[0].set(0).at[PROBES - 1].set(NPIX - 1)
    return jnp.stack([row_coord, column_coord], axis=1)


def set_ends(array, stream_key, least, largest):
    longest = array.shape.index(max(array.shape))
    spots = []
    for shift in (0, 1):
        where = [jax.random.randint(jax.random.fold_in(stream_key, axis), (), 0, length) for axis, length in enumerate(array.shape)]
        where[longest] = (where[longest] + shift) % array.shape[longest]
        spots.append(tuple(where))
    return array.at[spots[0]].set(least).at[spots[1]].set(largest)


def block_scale(stream_key, dims, cuts, least, high):
    gain = 1.0
    for dim, parts in cuts:
        steps = jax.random.uniform(jax.random.fold_in(jax.random.fold_in(stream_key, 6), dim), (parts,), jnp.float32, least / len(cuts), high / len(cuts))
        gain = gain * jnp.repeat(jnp.exp(steps), dims[dim] // parts).reshape((-1,) + (1,) * (len(dims) - 1 - dim))
    return gain


def setup_inputs(seed: int = 0) -> dict:
    key_of = jax.random.split(jax.random.key(seed), 8)
    tilts = set_ends(jax.random.randint(key_of[0], (BEAMS, 2), 0 - NPIX // 16, NPIX // 16 + 1), jax.random.fold_in(key_of[0], 1), 0 - NPIX // 16, (NPIX // 16 + 1) - 1).astype(jnp.int32)
    potentials = jnp.clip(2.0 * jax.random.uniform(key_of[1], (TILES, NPIX, NPIX), jnp.float32) ** block_scale(key_of[1], (TILES, NPIX, NPIX), ((0, 64), (1, 2)), -0.2, 0.2), 0.0, 2.0).astype(jnp.bfloat16)
    owners = jax.random.randint(key_of[2], (SLICES,), 0, TILES).astype(jnp.int32)
    beam_amplitude = jnp.clip(0.5 + 1.0 * jax.random.uniform(key_of[3], (BEAMS,), jnp.float32) ** block_scale(key_of[3], (BEAMS,), ((0, 64),), -0.2, 0.2), 0.5, 1.5)
    beam_phase = jnp.clip(jax.random.uniform(key_of[4], (BEAMS,), jnp.float32, -3.140625, 3.140625), -3.140625, 3.140625)
    probe_positions = draw_probe_positions(jax.random.fold_in(key_of[7], 71), 0)
    beam_offsets = set_ends(jax.random.randint(key_of[6], (PROBES,), 0, BEAMS), jax.random.fold_in(key_of[6], 1), 0, BEAMS - 1).astype(jnp.int32)
    return dict(tilts=tilts, potentials=potentials, owners=owners, beam_amplitude=beam_amplitude, beam_phase=beam_phase, probe_positions=probe_positions, beam_offsets=beam_offsets)


ROW_CHIRP = 0.07

def fresnel_matrix(pixel_count):
    frequency = np.arange(pixel_count) - pixel_count // 2
    passband = (np.abs(frequency) * 3 <= pixel_count) * 1.0
    phases = -6.0 * math.pi * (3.0 * frequency / pixel_count) ** 2
    spec_real = passband * np.cos(phases)
    spec_imag = passband * np.sin(phases)
    steps_n = np.arange(pixel_count)
    turns = np.mod(frequency[:, None] * steps_n[None, :], pixel_count) * (2.0 * math.pi / pixel_count)
    cos_table = np.cos(turns)
    sin_table = np.sin(turns)
    kernel_real = (spec_real @ cos_table - spec_imag @ sin_table) / pixel_count
    kernel_imag = (spec_real @ sin_table + spec_imag @ cos_table) / pixel_count
    distance = (np.arange(pixel_count)[None, :] - np.arange(pixel_count)[:, None]) % pixel_count
    circ_real = kernel_real[distance]
    circ_imag = kernel_imag[distance]
    upper_half = np.concatenate([circ_real, circ_imag], axis=1)
    lower_half = np.concatenate([-circ_imag, circ_real], axis=1)
    return np.concatenate([upper_half, lower_half], axis=0).astype(jnp.float32)

def row_taps(radius):
    distance = np.arange(-radius, radius + 1) * 1.0
    envelope = np.exp(-0.5 * (distance / radius) ** 2)
    angle_table = math.pi * ROW_CHIRP * distance ** 2
    norm_value = np.sqrt(np.sum(envelope ** 2))
    taps_real = envelope * np.cos(angle_table) / norm_value
    taps_imag = envelope * np.sin(angle_table) / norm_value
    return ([float(entry) for entry in taps_real], [float(entry) for entry in taps_imag])

def plane_waves(tilt_table, row_start, row_count, pixel_count):
    row_ids = row_start + jnp.arange(row_count, dtype=jnp.int32)
    column_ids = jnp.arange(pixel_count, dtype=jnp.int32)
    turns = jnp.mod(tilt_table[:, 0][:, None, None] * row_ids[None, :, None] + tilt_table[:, 1][:, None, None] * column_ids[None, None, :], pixel_count)
    angles = turns.astype(jnp.float32) * (2.0 * math.pi / pixel_count)
    return jnp.concatenate([jnp.cos(angles), jnp.sin(angles)], axis=2)

def transmission(potential_tile):
    phases = potential_tile.astype(jnp.float32)
    return jnp.concatenate([jnp.cos(phases), jnp.sin(phases)], axis=-1).astype(jnp.bfloat16)

def transmit(wavefield, factor):
    pixel_count = wavefield.shape[-1] // 2
    wave_real = wavefield[..., :pixel_count]
    wave_imag = wavefield[..., pixel_count:]
    factor_real = factor[..., :pixel_count].astype(jnp.float32)
    factor_imag = factor[..., pixel_count:].astype(jnp.float32)
    product = jnp.concatenate([wave_real * factor_real - wave_imag * factor_imag, wave_real * factor_imag + wave_imag * factor_real], axis=-1)
    return product.astype(jnp.bfloat16)

def mix_rows(spread, taps_real, taps_imag):
    pixel_count = spread.shape[-1] // 2
    radius = (len(taps_real) - 1) // 2
    total_real = jnp.zeros(spread[:, :pixel_count].shape, jnp.float32)
    total_imag = jnp.zeros(spread[:, :pixel_count].shape, jnp.float32)
    for position in range(len(taps_real)):
        moved = jnp.roll(spread, position - radius, axis=0)
        moved_real = moved[:, :pixel_count]
        moved_imag = moved[:, pixel_count:]
        total_real = total_real + taps_real[position] * moved_real - taps_imag[position] * moved_imag
        total_imag = total_imag + taps_real[position] * moved_imag + taps_imag[position] * moved_real
    return jnp.concatenate([total_real, total_imag], axis=1)

def coefficients(tilt_table, beam_ids, amplitude, phase, position, offset_value, beam_count, span, pixel_count):
    turns = jnp.mod(tilt_table[:, 0] * position[0] + tilt_table[:, 1] * position[1], pixel_count)
    angles = phase - turns.astype(jnp.float32) * (2.0 * math.pi / pixel_count)
    inside = (jnp.mod(beam_ids - offset_value, beam_count) < span).astype(jnp.float32)
    weight = amplitude * inside * (1.0 / math.sqrt(span))
    return (weight * jnp.cos(angles), weight * jnp.sin(angles))

def combine(coeff_real, coeff_imag, real_window, imag_window):
    probe_real = jnp.einsum('b,bjk->jk', coeff_real, real_window) - jnp.einsum('b,bjk->jk', coeff_imag, imag_window)
    probe_imag = jnp.einsum('b,bjk->jk', coeff_real, imag_window) + jnp.einsum('b,bjk->jk', coeff_imag, real_window)
    return jnp.concatenate([probe_real, probe_imag], axis=1)

def reference(tilts, potentials, owners, beam_amplitude, beam_phase, probe_positions, beam_offsets):
    pixel_count = potentials.shape[1]
    matrix = jnp.asarray(fresnel_matrix(pixel_count)).astype(jnp.bfloat16)
    matrix = lax.optimization_barrier(matrix).astype(jnp.float32)
    taps_real, taps_imag = row_taps(RAD)
    factors = []
    for layer_index in range(SLICES):
        potential_tile = lax.dynamic_index_in_dim(potentials, owners[layer_index], 0, keepdims=False)
        factors.append(lax.optimization_barrier(transmission(potential_tile)))

    def one_beam(tilt_row):
        wavefield = plane_waves(tilt_row[None, :], jnp.int32(0), pixel_count, pixel_count)[0]
        for layer_index in range(SLICES):
            transmitted = lax.optimization_barrier(transmit(wavefield, factors[layer_index]))
            spread = jnp.dot(transmitted.astype(jnp.float32), matrix, preferred_element_type=jnp.float32)
            wavefield = mix_rows(spread, taps_real, taps_imag)
        return wavefield.astype(jnp.bfloat16)
    exit_waves = lax.map(one_beam, tilts)
    beam_count = tilts.shape[0]
    span = beam_count // 2
    beam_ids = jnp.arange(beam_count, dtype=jnp.int32)

    def one_probe(inputs):
        position, offset_value = inputs
        coeff_real, coeff_imag = coefficients(tilts, beam_ids, beam_amplitude, beam_phase, position, offset_value, beam_count, span, pixel_count)
        row_ids = jnp.mod(position[0] + jnp.arange(WIN, dtype=jnp.int32), pixel_count)
        column_ids = jnp.mod(position[1] + jnp.arange(WIN, dtype=jnp.int32), pixel_count)
        picked = jnp.take(exit_waves, row_ids, axis=1)
        real_window = jnp.take(picked[:, :, :pixel_count], column_ids, axis=2).astype(jnp.float32)
        imag_window = jnp.take(picked[:, :, pixel_count:], column_ids, axis=2).astype(jnp.float32)
        return combine(coeff_real, coeff_imag, real_window, imag_window)
    probe_waves = lax.map(one_probe, (probe_positions, beam_offsets))
    return (exit_waves, probe_waves.reshape(N_ROW, PROBE_BLOCK, WIN, 2 * WIN))
```

```python
import math

import jax
import jax.numpy as jnp
import ml_dtypes
import numpy as np
from jax import lax
from jax.experimental import pallas as pl
from jax.experimental.pallas import tpu as pltpu
from jax.sharding import PartitionSpec as P

NPIX = 1024
RAD = 8
WIN = 64
ROW_CHIRP = 0.07
QUARTER = NPIX // 4
LANES = 128
STRIPS = NPIX // LANES
BEFORE = 2 * RAD
AFTER = 80
KEPT = BEFORE + NPIX // 2 + AFTER
BLOCK_IN = 128
BLOCK = BLOCK_IN - 2 * RAD
FULL_BLOCKS = 4
TAIL = FULL_BLOCKS * BLOCK
PASSED = TAIL + BLOCK_IN - 6 * RAD
STEP = 48
F32 = jnp.float32
BF16 = jnp.bfloat16
MESH = pl.DeviceIdType.MESH


def row_taps():
    distance = np.arange(-RAD, RAD + 1) * 1.0
    envelope = np.exp(-0.5 * (distance / RAD) ** 2)
    angles = math.pi * ROW_CHIRP * distance**2
    norm = np.sqrt(np.sum(envelope**2))
    return envelope * np.cos(angles) / norm, envelope * np.sin(angles) / norm


def row_matrices():
    taps_real, taps_imag = row_taps()
    real = np.zeros((BLOCK, BLOCK_IN))
    imag = np.zeros((BLOCK, BLOCK_IN))
    for out in range(BLOCK):
        for position in range(2 * RAD + 1):
            offset = position - RAD
            real[out, out + RAD - offset] = taps_real[position]
            imag[out, out + RAD - offset] = taps_imag[position]
    return real.astype(np.float32), imag.astype(np.float32)


def ring_matrices():
    frequency = np.arange(NPIX) - NPIX // 2
    passband = (np.abs(frequency) * 3 <= NPIX) * 1.0
    phases = -6.0 * math.pi * (3.0 * frequency / NPIX) ** 2
    turns = np.mod(frequency[:, None] * np.arange(NPIX)[None, :], NPIX) * (2.0 * math.pi / NPIX)
    spectrum = passband * np.exp(1j * phases)
    kernel = (spectrum @ np.exp(1j * turns)) / NPIX
    held_real = kernel.real.astype(np.float32).astype(ml_dtypes.bfloat16).astype(np.float64)
    held_imag = kernel.imag.astype(np.float32).astype(ml_dtypes.bfloat16).astype(np.float64)
    quarters = (held_real + 1j * held_imag).reshape(4, QUARTER)
    steps = np.arange(QUARTER)[None, :] - np.arange(QUARTER)[:, None]
    matrices = []
    for ring in range(4):
        root = 1j**ring
        folded = sum(root**part * quarters[part] for part in range(4)) / 4.0
        matrix = np.where(steps >= 0, 1.0, root) * folded[steps % QUARTER]
        matrices.append(
            np.block([[matrix.real, matrix.imag], [-matrix.imag, matrix.real]]).astype(np.float32)
        )
    return np.stack(matrices).astype(ml_dtypes.bfloat16)


def fitted(function, degree, reach=1.0):
    nodes = reach * np.cos(np.pi * (np.arange(64) + 0.5) / 64)
    powers = np.stack([nodes**power for power in degree], axis=1)
    return [float(c) for c in np.linalg.lstsq(powers, function(nodes), rcond=None)[0]]


def polynomial(coefficients, square):
    total = coefficients[-1]
    for c in coefficients[-2::-1]:
        total = total * square + c
    return total


EVEN = fitted(np.cos, (0, 2, 4, 6, 8))
ODD = fitted(np.sin, (1, 3, 5, 7))
TURN_EVEN = fitted(lambda u: np.cos(2 * np.pi * u), range(0, 17, 2), 0.5)
TURN_ODD = fitted(lambda u: np.sin(2 * np.pi * u), range(1, 18, 2), 0.5)


def circle(turns):
    square = turns * turns
    return polynomial(TURN_EVEN, square), polynomial(TURN_ODD, square) * turns


def phasor(steps):
    return circle((((steps + NPIX // 2) & (NPIX - 1)) - NPIX // 2).astype(F32) * (1.0 / NPIX))


def cos_sin(values):
    shifted = values - 1.0
    square = shifted * shifted
    even = polynomial(EVEN, square)
    odd = polynomial(ODD, square) * shifted
    c1, s1 = math.cos(1.0), math.sin(1.0)
    return c1 * even - s1 * odd, s1 * even + c1 * odd


def dot(a, b):
    return jnp.dot(a, b, preferred_element_type=F32)


def split(real, imag):
    r = [real[:, q * QUARTER : (q + 1) * QUARTER] for q in range(4)]
    i = [imag[:, q * QUARTER : (q + 1) * QUARTER] for q in range(4)]
    ar, ai, br, bi = r[0] + r[2], i[0] + i[2], r[0] - r[2], i[0] - i[2]
    cr, ci, dr, di = r[1] + r[3], i[1] + i[3], r[1] - r[3], i[1] - i[3]
    pairs = ((ar + cr, ai + ci), (br - di, bi + dr), (ar - cr, ai - ci), (br + di, bi - dr))
    return [jnp.concatenate([p.astype(BF16), q.astype(BF16)], axis=1) for p, q in pairs]


def join(products):
    r = [p[:, :QUARTER] for p in products]
    i = [p[:, QUARTER:] for p in products]
    ar, ai, br, bi = r[0] + r[2], i[0] + i[2], r[0] - r[2], i[0] - i[2]
    cr, ci, dr, di = r[1] + r[3], i[1] + i[3], r[1] - r[3], i[1] - i[3]
    return ((ar + cr, ai + ci), (br + di, bi - dr), (ar - cr, ai - ci), (br - di, bi + dr))


def propagate(parts, rings):
    return join([dot(jnp.concatenate(p, axis=0), rings[j]) for j, p in enumerate(zip(*parts))])


def first_kernel(
    owners,
    tilts,
    amplitude,
    angle,
    positions,
    offsets,
    tiles,
    taps_real,
    taps_imag,
    taps,
    rings_held,
    passed_out,
    field_out,
    beams,
    own,
    other,
    sent,
    masked,
    arrived1,
    summed1,
    arrived2,
    summed2,
    arrived3,
    after_in,
    before_in,
    kept,
    rings,
    factor0,
    factor1,
    beam_taps,
    phase,
    incident,
    field,
    passed,
    load_sem,
    swap_send,
    swap_recv,
    send_sem,
    recv_sem,
    edge_send,
    edge_recv,
    beam_send,
    beam_recv,
    store_sem,
):
    me, block = lax.axis_index("beam"), lax.axis_index("row")
    core = me % 2
    x, y, z = me // 2 % 4, me // 8 % 4, me // 32
    half = STRIPS // 2
    rows = tiles.shape[1]
    piece = rows // 4
    probe_id = block * lax.axis_size("beam") + me
    row_start = block * rows
    probe_row = positions[0, probe_id] - row_start
    probe_column = positions[1, probe_id]

    def at(x, y, z, core):
        return ((z * 4 + y) * 4 + x) * 2 + core

    twin = at(x, y, z, 1 - core)
    facing = at(x, y, 1 - z, core)
    along_x = [at((x + k) % 4, y, z, core) for k in (1, 2, 3)]
    along_y = [at(x, (y + k) % 4, z, core) for k in (1, 2, 3)]
    place1 = x * (1 - core) + y * core
    place2 = y * (1 - core) + x * core
    line1 = [at((x + k * (1 - core)) % 4, (y + k * core) % 4, z, core) for k in (1, 2, 3)]
    line2 = [at((x + k * core) % 4, (y + k * (1 - core)) % 4, z, core) for k in (1, 2, 3)]

    loads = []
    for strip in range(half):
        for group, target in enumerate((own, sent)):
            side = core if group == 0 else 1 - core
            column = pl.multiple_of((side * half + strip) * LANES, LANES)
            loads.append(
                pltpu.make_async_copy(
                    tiles.at[0, :, pl.ds(column, LANES)],
                    target.at[strip],
                    load_sem.at[group * half + strip],
                )
            )
    loads.append(pltpu.make_async_copy(rings_held, rings, load_sem.at[STRIPS]))
    for load in loads:
        load.start()

    barrier = pltpu.get_barrier_semaphore()
    partners = [(twin, block), (facing, block), (me, 1 - block), (facing, 1 - block)]
    partners += [(b, block) for b in along_x + along_y]
    for partner in partners:
        pl.semaphore_signal(barrier, inc=1, device_id=partner, device_id_type=MESH)

    lane = lax.broadcasted_iota(jnp.int32, (1, 1, LANES), 2)
    payload = jnp.zeros((1, 1, LANES), F32)
    for beam in range(2):
        values = (
            tilts[beam, 0].astype(F32),
            tilts[beam, 1].astype(F32),
            amplitude[beam],
            angle[beam],
        )
        for n, value in enumerate(values):
            payload = jnp.where(lane == 4 * beam + n, value, payload)
    beams[pl.ds(me, 1)] = payload

    for beam in range(2):
        tilt_row, tilt_column = tilts[beam, 0], tilts[beam, 1]
        pc, ps = phasor(tilt_row * lax.broadcasted_iota(jnp.int32, (8, BLOCK_IN), 1))
        pc, ps = pc[:1], ps[:1]
        real = taps_real[...] * pc - taps_imag[...] * ps
        imag = taps_real[...] * ps + taps_imag[...] * pc
        low = 2 * BLOCK * beam
        beam_taps[low : low + BLOCK, :] = jnp.concatenate([real, -imag], axis=1).astype(BF16)
        low += BLOCK
        beam_taps[low : low + BLOCK, :] = jnp.concatenate([imag, real], axis=1).astype(BF16)
        starts = row_start - BEFORE + BLOCK * lax.broadcasted_iota(jnp.int32, (8, NPIX), 0)
        pc, ps = phasor(
            tilt_row * starts + tilt_column * lax.broadcasted_iota(jnp.int32, (8, NPIX), 1)
        )
        phase[beam, 0] = pc
        phase[beam, 1] = ps

    pl.semaphore_wait(barrier, len(partners))
    started = []

    def copy_of(source, target, send_at, recv_at, device):
        return pltpu.make_async_remote_copy(
            src_ref=source,
            dst_ref=target,
            send_sem=send_at,
            recv_sem=recv_at,
            device_id=device,
            device_id_type=MESH,
        )

    def send(*args):
        copy = copy_of(*args)
        copy.start()
        started.append(copy)
        return copy

    def beam_chunk(size):
        return beams.at[pl.ds(pl.multiple_of(me // size * size, size), size)]

    chunk = beam_chunk(1)
    beam_copies = [send(chunk, chunk, beam_send.at[0], beam_recv.at[0], (twin, block))]
    for load in loads[:STRIPS]:
        load.wait()
    swap = send(sent, other, swap_send.at[0], swap_recv.at[0], (twin, block))

    def beam_step(size, devices, slot):
        for copy in beam_copies:
            copy.wait_recv()
        chunk = beam_chunk(size)
        beam_copies[:] = [
            send(chunk, chunk, beam_send.at[slot + k], beam_recv.at[slot + k], (device, block))
            for k, device in enumerate(devices)
        ]

    beam_step(2, along_x, 1)
    swap.wait_recv()

    copies = [None, None]
    for s in range(2):
        keep_own = jnp.where(owners[s] == me, 1.0, 0.0)
        keep_other = jnp.where(owners[s] == twin, 1.0, 0.0)
        for strip in range(half):
            value = own[strip].astype(F32) * keep_own + other[strip].astype(F32) * keep_other
            masked[s, strip] = value.astype(BF16)
        copies[s] = [
            send(
                masked.at[s, (place1 + k + 1) % 4],
                arrived1.at[s, k],
                send_sem.at[s, k],
                recv_sem.at[s, k],
                (line1[k], block),
            )
            for k in range(3)
        ]
    beam_step(8, along_y, 4)
    for s in range(2):
        for copy in copies[s]:
            copy.wait_recv()
        total = masked[s, place1].astype(F32)
        for k in range(3):
            total += arrived1[s, k].astype(F32)
        summed1[s] = total.astype(BF16)
        copies[s] = [
            send(
                summed1.at[s, pl.ds(pl.multiple_of((place2 + k + 1) % 4 * piece, piece), piece)],
                arrived2.at[s, k],
                send_sem.at[s, k + 3],
                recv_sem.at[s, k + 3],
                (line2[k], block),
            )
            for k in range(3)
        ]
    beam_step(32, [facing], 7)

    edge_to = [(me, 1 - block), (facing, 1 - block)]
    edges = [
        (0, pl.ds(0, AFTER), after_in, pl.ds(BEFORE + rows, AFTER)),
        (3, pl.ds(piece - BEFORE, BEFORE), before_in, pl.ds(0, BEFORE)),
    ]

    def edge_copies(s, n):
        _, source, target, _ = edges[n]
        return [
            copy_of(
                summed2.at[s, source],
                target.at[s, k],
                edge_send.at[s, n, k],
                edge_recv.at[s, n, k],
                edge_to[k],
            )
            for k in range(2)
        ]

    def edge_spread(s, n, peers=range(3)):
        place = kept.at[s, strip, edges[n][3]]
        return [
            copy_of(
                place, place, edge_send.at[s, n, k + 2], edge_recv.at[s, n, 2], (line2[k], block)
            )
            for k in peers
        ]

    mine = pl.ds(pl.multiple_of(place2 * piece, piece), piece)
    mine_kept = pl.ds(pl.multiple_of(place2 * piece + BEFORE, BEFORE), piece)
    strip = core * half + place1
    for s in range(2):
        for copy in copies[s]:
            copy.wait_recv()
        total = summed1[s, mine].astype(F32)
        for k in range(3):
            total += arrived2[s, k].astype(F32)
        summed2[s] = total.astype(BF16)
        copies[s] = [
            send(
                summed2.at[s],
                arrived3.at[s],
                send_sem.at[s, 6],
                recv_sem.at[s, 6],
                (facing, block),
            )
        ]
        for n in range(2):

            @pl.when(place2 == edges[n][0])
            def _(s=s, n=n):
                for copy in edge_copies(s, n):
                    copy.start()

    def back_along_second(s):
        copies[s][0].wait_recv()
        kept[s, strip, mine_kept] = (
            summed2[s].astype(F32) + arrived3[s].astype(F32)
        ).astype(BF16)
        place = kept.at[s, strip, mine_kept]
        copies[s] = [
            send(place, place, send_sem.at[s, k + 7], recv_sem.at[s, k + 7], (line2[k], block))
            for k in range(3)
        ]
        for n in range(2):

            @pl.when(place2 == edges[n][0])
            def _(n=n):
                for copy in edge_copies(s, n):
                    copy.wait_recv()
                arrived = edges[n][2]
                total = arrived[s, 0].astype(F32) + arrived[s, 1].astype(F32)
                kept[s, strip, edges[n][3]] = total.astype(BF16)
                for copy in edge_spread(s, n):
                    copy.start()

    def back_along_first(s):
        for copy in copies[s]:
            copy.wait_recv()
        for n in range(2):

            @pl.when(place2 != edges[n][0])
            def _(n=n):
                edge_spread(s, n, [0])[0].wait_recv()

        place = kept.at[s, strip]
        copies[s] = [
            send(place, place, send_sem.at[s, k + 10], recv_sem.at[s, k + 10], (line1[k], block))
            for k in range(3)
        ]

    def back_to_twin(s):
        for copy in copies[s]:
            copy.wait_recv()
        place = kept.at[s, pl.ds(pl.multiple_of(core * half, half), half)]
        copies[s] = [send(place, place, send_sem.at[s, 13], recv_sem.at[s, 13], (twin, block))]

    back_along_second(0)
    back_along_second(1)
    back_along_first(0)

    for copy in beam_copies:
        copy.wait_recv()
    reach = BLOCK_IN - 4 * RAD
    table = beams[...].reshape(beams.shape[0], LANES)
    both = jnp.concatenate([table[:, 0:4], table[:, 4:8]], axis=0)
    count = both.shape[0]
    ids = lax.broadcasted_iota(jnp.int32, (count, 1), 0)
    ids = jnp.where(ids < count // 2, 2 * ids, 2 * ids - count + 1)
    ky = both[:, 0:1].astype(jnp.int32)
    kx = both[:, 1:2].astype(jnp.int32)
    inside = (((ids - offsets[probe_id] + count) & (count - 1)) < count // 2).astype(F32)
    weight = both[:, 2:3] * inside * (1.0 / math.sqrt(count // 2))
    angle_c, angle_s = circle(both[:, 3:4] * (0.5 / math.pi))
    rel = lax.broadcasted_iota(jnp.int32, (count, LANES), 1) - BEFORE
    pc, ps = phasor(ky * rel - kx * probe_column)
    left_real = weight * (angle_c * pc - angle_s * ps)
    left_imag = weight * (angle_s * pc + angle_c * ps)
    left_real, left_imag = left_real.T[:reach], left_imag.T[:reach]
    left = jnp.concatenate(
        [
            jnp.concatenate([left_real, -left_imag], axis=1),
            jnp.concatenate([left_imag, left_real], axis=1),
        ],
        axis=0,
    )
    high = left.astype(BF16)
    left = jnp.concatenate([high, (left - high.astype(F32)).astype(BF16)], axis=0)
    pc, ps = phasor(kx * lax.broadcasted_iota(jnp.int32, (count, LANES), 1))
    qc, qs = phasor(kx * (LANES * lax.broadcasted_iota(jnp.int32, (count, STRIPS), 1)))
    for pair in range(STRIPS // 2):
        right = []
        for n in (2 * pair, 2 * pair + 1):
            c, s = qc[:, n : n + 1], qs[:, n : n + 1]
            right.append(jnp.concatenate([pc * c - ps * s, pc * s + ps * c], axis=0).astype(BF16))
        wave = dot(left, jnp.concatenate(right, axis=1))
        columns = slice(pair * 2 * LANES, (pair + 1) * 2 * LANES)
        incident[:, columns] = wave[: 2 * reach] + wave[2 * reach :]

    back_along_first(1)
    back_to_twin(0)

    def window(s, first, count, pair):
        chosen = lax.broadcasted_iota(jnp.int32, (count, KEPT), 0) + first
        chosen = (lax.broadcasted_iota(jnp.int32, (count, KEPT), 1) == chosen).astype(BF16)
        held = jnp.concatenate([kept[s, 2 * pair], kept[s, 2 * pair + 1]], axis=1)
        c, s = cos_sin(dot(chosen, held))
        return c.astype(BF16).astype(F32), s.astype(BF16).astype(F32)

    copies[0][0].wait_recv()

    def factors0(step, carry):
        held = pl.ds(pl.multiple_of(step * STEP, 16), STEP)
        for strip in range(STRIPS):
            columns = slice(strip * LANES, (strip + 1) * LANES)
            c, s = cos_sin(kept[0, strip, held, :].astype(F32))
            factor0[0, held, columns] = c.astype(BF16)
            factor0[1, held, columns] = s.astype(BF16)
        return carry

    lax.fori_loop(0, factor0.shape[1] // STEP, factors0, 0)
    back_to_twin(1)
    field[...] = jnp.zeros(field.shape, BF16)
    for pair in range(STRIPS // 2):
        columns = slice(pair * QUARTER, (pair + 1) * QUARTER)
        fr, fi = window(0, probe_row, reach, pair)
        r, i = incident[:reach, columns], incident[reach:, columns]
        field[:reach, columns] = (r * fr - i * fi).astype(BF16)
        field[BLOCK_IN : BLOCK_IN + reach, columns] = (r * fi + i * fr).astype(BF16)

    copies[1][0].wait_recv()

    def factors1(step, carry):
        start = pl.multiple_of(step * STEP, 16)
        for strip in range(STRIPS):
            columns = slice(strip * LANES, (strip + 1) * LANES)
            values = kept[1, strip, pl.ds(start, STEP + 16), :].astype(F32)[RAD : RAD + STEP]
            c, s = cos_sin(values)
            factor1[0, pl.ds(start, STEP), columns] = c.astype(BF16)
            factor1[1, pl.ds(start, STEP), columns] = s.astype(BF16)
        return carry

    lax.fori_loop(0, factor1.shape[1] // STEP, factors1, 0)
    loads[STRIPS].wait()

    def turned(mixed, count, beam, block):
        real, imag = mixed[:count], mixed[count:]
        pc = phase[beam, 0, pl.ds(block, 1), :]
        ps = phase[beam, 1, pl.ds(block, 1), :]
        return split(real * pc - imag * ps, real * ps + imag * pc)

    def pass_on(quarters, start, count):
        for q, (real, imag) in enumerate(quarters):
            columns = slice(q * QUARTER, (q + 1) * QUARTER)
            fr = factor1[0, pl.ds(start, count), columns].astype(F32)
            fi = factor1[1, pl.ds(start, count), columns].astype(F32)
            for beam in range(2):
                r, i = real[beam * count : (beam + 1) * count], imag[beam * count : (beam + 1) * count]
                passed[beam, 0, pl.ds(start, count), columns] = (r * fr - i * fi).astype(BF16)
                passed[beam, 1, pl.ds(start, count), columns] = (r * fi + i * fr).astype(BF16)

    def store(n, start, count):
        part = pl.ds(start, count)
        return pltpu.make_async_copy(
            passed.at[:, :, part], passed_out.at[:, :, part], store_sem.at[n]
        )

    def block_of(start):
        return jnp.concatenate(
            [factor0[0, pl.ds(start, BLOCK_IN), :], factor0[1, pl.ds(start, BLOCK_IN), :]], axis=0
        )

    def first_block(block, carry):
        start = pl.multiple_of(block * BLOCK, 16)
        mixed = dot(beam_taps[...], block_of(start))
        parts = [
            turned(mixed[2 * BLOCK * beam : 2 * BLOCK * (beam + 1)], BLOCK, beam, block)
            for beam in range(2)
        ]
        pass_on(propagate(parts, rings), start, BLOCK)
        store(block, start, BLOCK).start()
        return carry

    lax.fori_loop(0, FULL_BLOCKS, first_block, 0, unroll=2)

    out = PASSED - TAIL
    tops = [BLOCK * n for n in range(4)]
    left = jnp.concatenate([beam_taps[top : top + out] for top in tops])
    mixed = dot(left, block_of(TAIL))
    parts = [
        turned(mixed[2 * out * beam : 2 * out * (beam + 1)], out, beam, FULL_BLOCKS)
        for beam in range(2)
    ]
    mixed = dot(jnp.concatenate([taps[:out], taps[BLOCK : BLOCK + out]]), field[...])
    parts.append(split(mixed[:out], mixed[out:]))
    quarters = propagate(parts, rings)
    pass_on(quarters, TAIL, out)
    last = store(FULL_BLOCKS, TAIL, out)
    last.start()
    field[...] = jnp.zeros(field.shape, BF16)
    for pair, (real, imag) in enumerate(quarters):
        columns = slice(pair * QUARTER, (pair + 1) * QUARTER)
        r, i = real[2 * out :], imag[2 * out :]
        fr, fi = window(1, probe_row + RAD, out, pair)
        field[:out, columns] = (r * fr - i * fi).astype(BF16)
        field[BLOCK_IN : BLOCK_IN + out, columns] = (r * fi + i * fr).astype(BF16)
    field_copy = pltpu.make_async_copy(field, field_out, store_sem.at[FULL_BLOCKS + 1])
    field_copy.start()

    for copy in started:
        copy.wait_send()
    for s in range(2):
        for n in range(2):

            @pl.when(place2 == edges[n][0])
            def _(s=s, n=n):
                for copy in edge_copies(s, n) + edge_spread(s, n):
                    copy.wait_send()

    for n in range(FULL_BLOCKS):
        store(n, n * BLOCK, BLOCK).wait()
    last.wait()
    field_copy.wait()


def first_slice(owners, tilts, amplitude, angle, positions, offsets, tiles):
    real, imag = row_matrices()
    taps = np.block([[real, -imag], [imag, real]]).astype(ml_dtypes.bfloat16)
    half = STRIPS // 2
    rows = tiles.shape[1]
    piece = rows // 4
    vmem = pl.BlockSpec(memory_space=pltpu.VMEM)
    smem = pl.BlockSpec(memory_space=pltpu.SMEM)
    anywhere = pl.BlockSpec(memory_space=pl.ANY)
    reach = BLOCK_IN - 4 * RAD
    return pl.pallas_call(
        first_kernel,
        out_shape=(
            jax.ShapeDtypeStruct((2, 2, PASSED, NPIX), BF16),
            jax.ShapeDtypeStruct((2 * BLOCK_IN, NPIX), BF16),
        ),
        in_specs=[smem] * 6 + [anywhere] + [vmem] * 3 + [anywhere],
        out_specs=(anywhere, anywhere),
        scratch_shapes=[
            pltpu.VMEM((lax.axis_size("beam"), 1, LANES), F32),
            pltpu.VMEM((half, rows, LANES), BF16),
            pltpu.VMEM((half, rows, LANES), BF16),
            pltpu.VMEM((half, rows, LANES), BF16),
            pltpu.VMEM((2, half, rows, LANES), BF16),
            pltpu.VMEM((2, 3, rows, LANES), BF16),
            pltpu.VMEM((2, rows, LANES), BF16),
            pltpu.VMEM((2, 3, piece, LANES), BF16),
            pltpu.VMEM((2, piece, LANES), BF16),
            pltpu.VMEM((2, piece, LANES), BF16),
            pltpu.VMEM((2, 2, AFTER, LANES), BF16),
            pltpu.VMEM((2, 2, BEFORE, LANES), BF16),
            pltpu.VMEM((2, STRIPS, KEPT, LANES), BF16),
            pltpu.VMEM((4, 2 * QUARTER, 2 * QUARTER), BF16),
            pltpu.VMEM((2, TAIL + BLOCK_IN, NPIX), BF16),
            pltpu.VMEM((2, PASSED, NPIX), BF16),
            pltpu.VMEM((4 * BLOCK, 2 * BLOCK_IN), BF16),
            pltpu.VMEM((2, 2, 8, NPIX), F32),
            pltpu.VMEM((2 * reach, NPIX), F32),
            pltpu.VMEM((2 * BLOCK_IN, NPIX), BF16),
            pltpu.VMEM((2, 2, PASSED, NPIX), BF16),
            pltpu.SemaphoreType.DMA((STRIPS + 1,)),
            pltpu.SemaphoreType.DMA((1,)),
            pltpu.SemaphoreType.DMA((1,)),
            pltpu.SemaphoreType.DMA((2, 14)),
            pltpu.SemaphoreType.DMA((2, 14)),
            pltpu.SemaphoreType.DMA((2, 2, 5)),
            pltpu.SemaphoreType.DMA((2, 2, 3)),
            pltpu.SemaphoreType.DMA((8,)),
            pltpu.SemaphoreType.DMA((8,)),
            pltpu.SemaphoreType.DMA((FULL_BLOCKS + 2,)),
        ],
        compiler_params=pltpu.CompilerParams(
            collective_id=0, has_side_effects=True, vmem_limit_bytes=60 * 2**20
        ),
        name="first_slice",
    )(
        owners,
        tilts,
        amplitude,
        angle,
        positions,
        offsets,
        tiles,
        jnp.asarray(real),
        jnp.asarray(imag),
        jnp.asarray(taps),
        jnp.asarray(ring_matrices()),
    )


def second_kernel(
    positions, taps, rings, passed_in, field, exit_out, probe, passed, waves, load_sem, store_sem
):
    probe_id = lax.axis_index("row") * lax.axis_size("beam") + lax.axis_index("beam")
    loads = []
    end = 0
    for n in range(FULL_BLOCKS + 1):
        start, end = end, min(n * BLOCK + BLOCK_IN, PASSED)
        loads.append(
            pltpu.make_async_copy(
                passed_in.at[:, :, start:end], passed.at[:, :, start:end], load_sem.at[n]
            )
        )
        loads[n].start()
    spare = passed.shape[2] - PASSED
    passed[:, :, PASSED:, :] = jnp.zeros((2, 2, spare, NPIX), BF16)

    def block_of(beam, start):
        return jnp.concatenate(
            [passed[beam, 0, start : start + BLOCK_IN], passed[beam, 1, start : start + BLOCK_IN]],
            axis=0,
        )

    stores = []

    def write(quarters, start, count):
        for q, (real, imag) in enumerate(quarters):
            for beam in range(2):
                chosen = slice(beam * count, (beam + 1) * count)
                low = q * QUARTER
                waves[beam, start : start + count, low : low + QUARTER] = real[chosen].astype(BF16)
                low += NPIX
                waves[beam, start : start + count, low : low + QUARTER] = imag[chosen].astype(BF16)
        part = slice(start, start + count)
        stores.append(
            pltpu.make_async_copy(
                waves.at[:, part], exit_out.at[:, part], store_sem.at[len(stores)]
            )
        )
        stores[-1].start()

    for block in range(FULL_BLOCKS):
        loads[block].wait()
        start = block * BLOCK
        parts = []
        for beam in range(2):
            mixed = dot(taps[...], block_of(beam, start))
            parts.append(split(mixed[:BLOCK], mixed[BLOCK:]))
        write(propagate(parts, rings), start, BLOCK)

    loads[FULL_BLOCKS].wait()
    left = jnp.concatenate([taps[:WIN], taps[BLOCK : BLOCK + WIN]])
    parts = []
    for mixed in [dot(left, block_of(beam, TAIL)) for beam in range(2)] + [dot(left, field[...])]:
        parts.append(split(mixed[:WIN], mixed[WIN:]))
    quarters = propagate(parts, rings)
    write(quarters, TAIL, WIN)
    shift = (NPIX - positions[1, probe_id]) & (NPIX - 1)
    real = jnp.concatenate([real[2 * WIN :] for real, _ in quarters], axis=1)
    imag = jnp.concatenate([imag[2 * WIN :] for _, imag in quarters], axis=1)
    real = pltpu.roll(real, shift, 1)[:, :WIN]
    imag = pltpu.roll(imag, shift, 1)[:, :WIN]
    probe[0, 0] = jnp.concatenate([real, imag], axis=1)
    for copy in stores:
        copy.wait()


def second_slice(positions, passed, field):
    real, imag = row_matrices()
    taps = np.block([[real, -imag], [imag, real]]).astype(ml_dtypes.bfloat16)
    vmem = pl.BlockSpec(memory_space=pltpu.VMEM)
    smem = pl.BlockSpec(memory_space=pltpu.SMEM)
    anywhere = pl.BlockSpec(memory_space=pl.ANY)
    return pl.pallas_call(
        second_kernel,
        out_shape=(
            jax.ShapeDtypeStruct((2, NPIX // 2, 2 * NPIX), BF16),
            jax.ShapeDtypeStruct((1, 1, WIN, 2 * WIN), F32),
        ),
        in_specs=[smem, vmem, vmem, anywhere, vmem],
        out_specs=(anywhere, vmem),
        scratch_shapes=[
            pltpu.VMEM((2, 2, TAIL + BLOCK_IN, NPIX), BF16),
            pltpu.VMEM((2, NPIX // 2, 2 * NPIX), BF16),
            pltpu.SemaphoreType.DMA((FULL_BLOCKS + 1,)),
            pltpu.SemaphoreType.DMA((FULL_BLOCKS + 1,)),
        ],
        compiler_params=pltpu.CompilerParams(vmem_limit_bytes=60 * 2**20),
        name="second_slice",
    )(positions, jnp.asarray(taps), jnp.asarray(ring_matrices()), passed, field)


def body(tilts, potentials, owners, beam_amplitude, beam_phase, probe_positions, beam_offsets):
    positions = probe_positions.T
    passed, field = first_slice(
        owners, tilts, beam_amplitude, beam_phase, positions, beam_offsets, potentials
    )
    return second_slice(positions, passed, field)


def solution(mesh):
    return jax.shard_map(
        body,
        mesh=mesh,
        in_specs=(P("beam", None), P("beam", "row", None), P(), P("beam"), P("beam"), P(), P()),
        out_specs=(P("beam", "row", None), P("row", "beam", None, None)),
        check_vma=False,
    )
```

```python
import math

import jax
import jax.numpy as jnp
import ml_dtypes
import numpy as np
from jax import lax
from jax.experimental import pallas as pl
from jax.experimental.pallas import tpu as pltpu
from jax.sharding import PartitionSpec as P

NPIX = 1024
RAD = 8
WIN = 64
ROW_CHIRP = 0.07
RINGS = 8
QUARTER = NPIX // RINGS
LANES = 128
STRIPS = NPIX // LANES
BEFORE = 2 * RAD
AFTER = 80
KEPT = BEFORE + NPIX // 2 + AFTER
BLOCK_IN = 128
BLOCK = BLOCK_IN - 2 * RAD
FULL_BLOCKS = 4
TAIL = FULL_BLOCKS * BLOCK
PASSED = TAIL + BLOCK_IN - 6 * RAD
STEP = 48
F32 = jnp.float32
BF16 = jnp.bfloat16
MESH = pl.DeviceIdType.MESH


def row_taps():
    distance = np.arange(-RAD, RAD + 1) * 1.0
    envelope = np.exp(-0.5 * (distance / RAD) ** 2)
    angles = math.pi * ROW_CHIRP * distance**2
    norm = np.sqrt(np.sum(envelope**2))
    return envelope * np.cos(angles) / norm, envelope * np.sin(angles) / norm


def row_matrices():
    taps_real, taps_imag = row_taps()
    real = np.zeros((BLOCK, BLOCK_IN))
    imag = np.zeros((BLOCK, BLOCK_IN))
    for out in range(BLOCK):
        for position in range(2 * RAD + 1):
            offset = position - RAD
            real[out, out + RAD - offset] = taps_real[position]
            imag[out, out + RAD - offset] = taps_imag[position]
    return real.astype(np.float32), imag.astype(np.float32)


def ring_matrices():
    frequency = np.arange(NPIX) - NPIX // 2
    passband = (np.abs(frequency) * 3 <= NPIX) * 1.0
    phases = -6.0 * math.pi * (3.0 * frequency / NPIX) ** 2
    turns = np.mod(frequency[:, None] * np.arange(NPIX)[None, :], NPIX) * (2.0 * math.pi / NPIX)
    spectrum = passband * np.exp(1j * phases)
    kernel = (spectrum @ np.exp(1j * turns)) / NPIX
    held_real = kernel.real.astype(np.float32).astype(ml_dtypes.bfloat16).astype(np.float64)
    held_imag = kernel.imag.astype(np.float32).astype(ml_dtypes.bfloat16).astype(np.float64)
    quarters = (held_real + 1j * held_imag).reshape(RINGS, QUARTER)
    steps = np.arange(QUARTER)[None, :] - np.arange(QUARTER)[:, None]
    matrices = []
    for ring in range(RINGS):
        root = np.exp(2j * np.pi * ring / RINGS)
        folded = sum(root**part * quarters[part] for part in range(RINGS)) / RINGS
        matrix = np.where(steps >= 0, 1.0, root) * folded[steps % QUARTER]
        matrices.append(
            np.block([[matrix.real, matrix.imag], [-matrix.imag, matrix.real]]).astype(np.float32)
        )
    return np.stack(matrices).astype(ml_dtypes.bfloat16)


def fitted(function, degree, reach=1.0):
    nodes = reach * np.cos(np.pi * (np.arange(64) + 0.5) / 64)
    powers = np.stack([nodes**power for power in degree], axis=1)
    return [float(c) for c in np.linalg.lstsq(powers, function(nodes), rcond=None)[0]]


def polynomial(coefficients, square):
    total = coefficients[-1]
    for c in coefficients[-2::-1]:
        total = total * square + c
    return total


EVEN = fitted(np.cos, (0, 2, 4, 6))
ODD = fitted(np.sin, (1, 3, 5, 7))
TURN_EVEN = fitted(lambda u: np.cos(2 * np.pi * u), range(0, 17, 2), 0.5)
TURN_ODD = fitted(lambda u: np.sin(2 * np.pi * u), range(1, 18, 2), 0.5)


def circle(turns):
    square = turns * turns
    return polynomial(TURN_EVEN, square), polynomial(TURN_ODD, square) * turns


def phasor(steps):
    return circle((((steps + NPIX // 2) & (NPIX - 1)) - NPIX // 2).astype(F32) * (1.0 / NPIX))


def cos_sin(values):
    shifted = values - 1.0
    square = shifted * shifted
    even = polynomial(EVEN, square)
    odd = polynomial(ODD, square) * shifted
    c1, s1 = math.cos(1.0), math.sin(1.0)
    return c1 * even - s1 * odd, s1 * even + c1 * odd


def dot(a, b):
    return jnp.dot(a, b, preferred_element_type=F32)


HALF = math.sqrt(0.5)


def add(a, b):
    return a[0] + b[0], a[1] + b[1]


def less(a, b):
    return a[0] - b[0], a[1] - b[1]


def plus_i(a, b):
    return a[0] - b[1], a[1] + b[0]


def less_i(a, b):
    return a[0] + b[1], a[1] - b[0]


def split(real, imag):
    x = [
        tuple(f[:, q * QUARTER : (q + 1) * QUARTER] for f in (real, imag)) for q in range(RINGS)
    ]
    rings = [None] * RINGS
    for odd in range(2):
        a = [(less if odd else add)(x[q], x[q + 4]) for q in range(4)]
        if odd:
            a[1] = ((a[1][0] - a[1][1]) * HALF, (a[1][0] + a[1][1]) * HALF)
            a[3] = ((a[3][0] + a[3][1]) * -HALF, (a[3][0] - a[3][1]) * HALF)
            b, c = plus_i(a[0], a[2]), add(a[1], a[3])
            e, d = less_i(a[0], a[2]), less(a[1], a[3])
        else:
            b, c = add(a[0], a[2]), add(a[1], a[3])
            e, d = less(a[0], a[2]), less(a[1], a[3])
        rings[odd], rings[4 + odd] = add(b, c), less(b, c)
        rings[2 + odd], rings[6 + odd] = plus_i(e, d), less_i(e, d)
    return [jnp.concatenate([p.astype(BF16), q.astype(BF16)], axis=1) for p, q in rings]


def join(products):
    y = [(p[:, :QUARTER], p[:, QUARTER:]) for p in products]
    halves = []
    for odd in range(2):
        b, e = add(y[odd], y[4 + odd]), less(y[odd], y[4 + odd])
        c, d = add(y[2 + odd], y[6 + odd]), less(y[2 + odd], y[6 + odd])
        halves.append([add(b, c), less_i(e, d), less(b, c), plus_i(e, d)])
    even, o = halves
    o[1] = ((o[1][0] + o[1][1]) * HALF, (o[1][1] - o[1][0]) * HALF)
    o[3] = ((o[3][1] - o[3][0]) * HALF, (o[3][0] + o[3][1]) * -HALF)
    first = [add(even[0], o[0]), add(even[1], o[1]), less_i(even[2], o[2]), add(even[3], o[3])]
    last = [less(even[0], o[0]), less(even[1], o[1]), plus_i(even[2], o[2]), less(even[3], o[3])]
    return first + last


def propagate(parts, rings):
    return join([dot(jnp.concatenate(p, axis=0), rings[j]) for j, p in enumerate(zip(*parts))])


def first_kernel(
    owners,
    tilts,
    amplitude,
    angle,
    positions,
    offsets,
    tiles,
    taps_real,
    taps_imag,
    taps_held,
    rings_held,
    passed_out,
    field_out,
    beams,
    own,
    other,
    sent,
    masked,
    arrived1,
    summed1,
    arrived2,
    summed2,
    arrived3,
    after_in,
    before_in,
    kept,
    taps,
    rings,
    factor0,
    factor1,
    beam_taps,
    phase,
    incident,
    field,
    passed,
    load_sem,
    swap_send,
    swap_recv,
    send_sem,
    recv_sem,
    twin_send,
    twin_recv,
    edge_send,
    edge_recv,
    beam_send,
    beam_recv,
    store_sem,
):
    me, block = lax.axis_index("beam"), lax.axis_index("row")
    core = me % 2
    x, y, z = me // 2 % 4, me // 8 % 4, me // 32
    half = STRIPS // 2
    rows = tiles.shape[1]
    piece = rows // 4
    probe_id = block * lax.axis_size("beam") + me
    row_start = block * rows
    probe_row = positions[0, probe_id] - row_start
    probe_column = positions[1, probe_id]

    def at(x, y, z, core):
        return ((z * 4 + y) * 4 + x) * 2 + core

    twin = at(x, y, z, 1 - core)
    facing = at(x, y, 1 - z, core)
    along_x = [at((x + k) % 4, y, z, core) for k in (1, 2, 3)]
    along_y = [at(x, (y + k) % 4, z, core) for k in (1, 2, 3)]
    place1 = x * (1 - core) + y * core
    place2 = y * (1 - core) + x * core
    line1 = [at((x + k * (1 - core)) % 4, (y + k * core) % 4, z, core) for k in (1, 2, 3)]
    line2 = [at((x + k * core) % 4, (y + k * (1 - core)) % 4, z, core) for k in (1, 2, 3)]

    barrier = pltpu.get_barrier_semaphore()
    partners = [(twin, block), (facing, block), (me, 1 - block), (facing, 1 - block)]
    partners += [(b, block) for b in along_x + along_y]
    for partner in partners:
        pl.semaphore_signal(barrier, inc=1, device_id=partner, device_id_type=MESH)

    loads = []
    for group, target in enumerate((sent, own)):
        for strip in range(half):
            side = 1 - core if group == 0 else core
            column = pl.multiple_of((side * half + strip) * LANES, LANES)
            loads.append(
                pltpu.make_async_copy(
                    tiles.at[0, :, pl.ds(column, LANES)],
                    target.at[strip],
                    load_sem.at[group * half + strip],
                )
            )
    loads.append(pltpu.make_async_copy(rings_held, rings, load_sem.at[STRIPS]))
    loads.append(pltpu.make_async_copy(taps_held, taps, load_sem.at[STRIPS + 1]))
    for load in loads[:STRIPS]:
        load.start()

    lane = lax.broadcasted_iota(jnp.int32, (1, 1, LANES), 2)
    payload = jnp.zeros((1, 1, LANES), F32)
    for beam in range(2):
        values = (
            tilts[beam, 0].astype(F32),
            tilts[beam, 1].astype(F32),
            amplitude[beam],
            angle[beam],
        )
        for n, value in enumerate(values):
            payload = jnp.where(lane == 4 * beam + n, value, payload)
    beams[pl.ds(me, 1)] = payload

    for beam in range(2):
        tilt_row, tilt_column = tilts[beam, 0], tilts[beam, 1]
        pc, ps = phasor(tilt_row * lax.broadcasted_iota(jnp.int32, (8, BLOCK_IN), 1))
        pc, ps = pc[:1], ps[:1]
        real = taps_real[...] * pc - taps_imag[...] * ps
        imag = taps_real[...] * ps + taps_imag[...] * pc
        low = 2 * BLOCK * beam
        beam_taps[low : low + BLOCK, :] = jnp.concatenate([real, -imag], axis=1).astype(BF16)
        low += BLOCK
        beam_taps[low : low + BLOCK, :] = jnp.concatenate([imag, real], axis=1).astype(BF16)
        starts = row_start - BEFORE + BLOCK * lax.broadcasted_iota(jnp.int32, (8, NPIX), 0)
        pc, ps = phasor(
            tilt_row * starts + tilt_column * lax.broadcasted_iota(jnp.int32, (8, NPIX), 1)
        )
        phase[beam, 0] = pc
        phase[beam, 1] = ps

    pl.semaphore_wait(barrier, len(partners))
    started = []

    def copy_of(source, target, send_at, recv_at, device):
        return pltpu.make_async_remote_copy(
            src_ref=source,
            dst_ref=target,
            send_sem=send_at,
            recv_sem=recv_at,
            device_id=device,
            device_id_type=MESH,
        )

    def send(*args):
        copy = copy_of(*args)
        copy.start()
        started.append(copy)
        return copy

    def beam_chunk(size):
        return beams.at[pl.ds(pl.multiple_of(me // size * size, size), size)]

    chunk = beam_chunk(1)
    beam_copies = [send(chunk, chunk, beam_send.at[0], beam_recv.at[0], (twin, block))]
    swaps = []
    for strip in range(half):
        loads[strip].wait()
        swaps.append(
            send(
                sent.at[strip],
                other.at[strip],
                swap_send.at[strip],
                swap_recv.at[strip],
                (twin, block),
            )
        )
    for load in loads[half:STRIPS]:
        load.wait()
    for load in loads[STRIPS:]:
        load.start()

    def beam_step(size, devices, slot):
        for copy in beam_copies:
            copy.wait_recv()
        chunk = beam_chunk(size)
        beam_copies[:] = [
            send(chunk, chunk, beam_send.at[slot + k], beam_recv.at[slot + k], (device, block))
            for k, device in enumerate(devices)
        ]

    for swap in swaps:
        swap.wait_recv()

    copies = [None, None]

    def out_along_first(s):
        keep_own = jnp.where(owners[s] == me, 1.0, 0.0)
        keep_other = jnp.where(owners[s] == twin, 1.0, 0.0)
        for strip in range(half):
            value = own[strip].astype(F32) * keep_own + other[strip].astype(F32) * keep_other
            masked[s, strip] = value.astype(BF16)
        copies[s] = [
            send(
                masked.at[s, (place1 + k + 1) % 4],
                arrived1.at[s, k],
                send_sem.at[s, k],
                recv_sem.at[s, k],
                (line1[k], block),
            )
            for k in range(3)
        ]

    def out_along_second(s):
        for copy in copies[s]:
            copy.wait_recv()
        total = masked[s, place1].astype(F32)
        for k in range(3):
            total += arrived1[s, k].astype(F32)
        summed1[s] = total.astype(BF16)
        copies[s] = [
            send(
                summed1.at[s, pl.ds(pl.multiple_of((place2 + k + 1) % 4 * piece, piece), piece)],
                arrived2.at[s, k],
                send_sem.at[s, k + 3],
                recv_sem.at[s, k + 3],
                (line2[k], block),
            )
            for k in range(3)
        ]

    out_along_first(0)
    beam_step(2, along_x, 1)
    out_along_first(1)
    out_along_second(0)
    beam_step(8, along_y, 4)
    out_along_second(1)

    edge_to = [(me, 1 - block), (facing, 1 - block)]
    edges = [
        (0, pl.ds(0, AFTER), after_in, pl.ds(BEFORE + rows, AFTER)),
        (3, pl.ds(piece - BEFORE, BEFORE), before_in, pl.ds(0, BEFORE)),
    ]

    def edge_copies(s, n):
        _, source, target, _ = edges[n]
        return [
            copy_of(
                summed2.at[s, source],
                target.at[s, k],
                edge_send.at[s, n, k],
                edge_recv.at[s, n, k],
                edge_to[k],
            )
            for k in range(2)
        ]

    def edge_spread(s, n, peers=range(3)):
        place = kept.at[s, strip, edges[n][3]]
        return [
            copy_of(
                place, place, edge_send.at[s, n, k + 2], edge_recv.at[s, n, 2], (line2[k], block)
            )
            for k in peers
        ]

    mine = pl.ds(pl.multiple_of(place2 * piece, piece), piece)
    mine_kept = pl.ds(pl.multiple_of(place2 * piece + BEFORE, BEFORE), piece)
    strip = core * half + place1

    def out_to_facing(s):
        for copy in copies[s]:
            copy.wait_recv()
        total = summed1[s, mine].astype(F32)
        for k in range(3):
            total += arrived2[s, k].astype(F32)
        summed2[s] = total.astype(BF16)
        copies[s] = [
            send(
                summed2.at[s],
                arrived3.at[s],
                send_sem.at[s, 6],
                recv_sem.at[s, 6],
                (facing, block),
            )
        ]
        for n in range(2):

            @pl.when(place2 == edges[n][0])
            def _(n=n):
                for copy in edge_copies(s, n):
                    copy.start()

    def back_along_second(s):
        copies[s][0].wait_recv()
        kept[s, strip, mine_kept] = (
            summed2[s].astype(F32) + arrived3[s].astype(F32)
        ).astype(BF16)
        place = kept.at[s, strip, mine_kept]
        copies[s] = [
            send(place, place, send_sem.at[s, k + 7], recv_sem.at[s, k + 7], (line2[k], block))
            for k in range(3)
        ]
        for n in range(2):

            @pl.when(place2 == edges[n][0])
            def _(n=n):
                for copy in edge_copies(s, n):
                    copy.wait_recv()
                arrived = edges[n][2]
                total = arrived[s, 0].astype(F32) + arrived[s, 1].astype(F32)
                kept[s, strip, edges[n][3]] = total.astype(BF16)
                for copy in edge_spread(s, n):
                    copy.start()

        onward(s, mine_kept)

    def line_copy(s, k, held, at_strip):
        place = kept.at[s, at_strip, held]
        return copy_of(
            place, place, send_sem.at[s, k + 10], recv_sem.at[s, k + 10], (line1[k], block)
        )

    def onward(s, held):
        for k in range(3):
            line_copy(s, k, held, strip).start()

    def strip_to_twin(s, n, at_strip):
        place = kept.at[s, at_strip]
        twin_copies[s].append(
            send(place, place, twin_send.at[s, n], twin_recv.at[s, n], (twin, block))
        )

    twin_copies = [[], []]
    whole = pl.ds(0, KEPT)

    def back_along_first(s):
        for k in (0, 2, 1):
            copies[s][k].wait_recv()
            came = (place2 + 3 - k) % 4 * piece + BEFORE
            onward(s, pl.ds(pl.multiple_of(came, BEFORE), piece))
        for n in range(2):

            @pl.when(place2 != edges[n][0])
            def _(n=n):
                edge_spread(s, n, [0])[0].wait_recv()

            onward(s, edges[n][3])
        strip_to_twin(s, 3, strip)

    def back_to_twin(s):
        for k in (0, 2, 1):
            line_copy(s, k, whole, strip).wait_recv()
            strip_to_twin(s, k, core * half + (place1 + 3 - k) % 4)

    out_to_facing(0)
    beam_step(32, [facing], 7)
    out_to_facing(1)
    back_along_second(0)
    back_along_second(1)
    back_along_first(0)
    back_along_first(1)

    for copy in beam_copies:
        copy.wait_recv()
    reach = BLOCK_IN - 4 * RAD
    table = beams[...].reshape(beams.shape[0], LANES)
    both = jnp.concatenate([table[:, 0:4], table[:, 4:8]], axis=0)
    count = both.shape[0]
    ids = lax.broadcasted_iota(jnp.int32, (count, 1), 0)
    ids = jnp.where(ids < count // 2, 2 * ids, 2 * ids - count + 1)
    ky = both[:, 0:1].astype(jnp.int32)
    kx = both[:, 1:2].astype(jnp.int32)
    inside = (((ids - offsets[probe_id] + count) & (count - 1)) < count // 2).astype(F32)
    weight = both[:, 2:3] * inside * (1.0 / math.sqrt(count // 2))
    angle_c, angle_s = circle(both[:, 3:4] * (0.5 / math.pi))
    rel = lax.broadcasted_iota(jnp.int32, (count, LANES), 1) - BEFORE
    pc, ps = phasor(ky * rel - kx * probe_column)
    left_real = weight * (angle_c * pc - angle_s * ps)
    left_imag = weight * (angle_s * pc + angle_c * ps)
    left_real, left_imag = left_real.T[:reach], left_imag.T[:reach]
    left = jnp.concatenate(
        [
            jnp.concatenate([left_real, -left_imag], axis=1),
            jnp.concatenate([left_imag, left_real], axis=1),
        ],
        axis=0,
    )
    high = left.astype(BF16)
    left = jnp.concatenate([high, (left - high.astype(F32)).astype(BF16)], axis=0)
    pc, ps = phasor(kx * lax.broadcasted_iota(jnp.int32, (count, LANES), 1))
    qc, qs = phasor(kx * (LANES * lax.broadcasted_iota(jnp.int32, (count, STRIPS), 1)))
    for pair in range(STRIPS // 2):
        right = []
        for n in (2 * pair, 2 * pair + 1):
            c, s = qc[:, n : n + 1], qs[:, n : n + 1]
            right.append(jnp.concatenate([pc * c - ps * s, pc * s + ps * c], axis=0).astype(BF16))
        wave = dot(left, jnp.concatenate(right, axis=1))
        columns = slice(pair * 2 * LANES, (pair + 1) * 2 * LANES)
        incident[:, columns] = wave[: 2 * reach] + wave[2 * reach :]

    back_to_twin(0)

    def window(s, first, count, pair):
        chosen = lax.broadcasted_iota(jnp.int32, (count, KEPT), 0) + first
        chosen = (lax.broadcasted_iota(jnp.int32, (count, KEPT), 1) == chosen).astype(BF16)
        held = jnp.concatenate([kept[s, 2 * pair], kept[s, 2 * pair + 1]], axis=1)
        c, s = cos_sin(dot(chosen, held))
        return c.astype(BF16).astype(F32), s.astype(BF16).astype(F32)

    for copy in twin_copies[0]:
        copy.wait_recv()

    def factors0(step, carry):
        held = pl.ds(pl.multiple_of(step * STEP, 16), STEP)
        for strip in range(STRIPS):
            columns = slice(strip * LANES, (strip + 1) * LANES)
            c, s = cos_sin(kept[0, strip, held, :].astype(F32))
            factor0[0, held, columns] = c.astype(BF16)
            factor0[1, held, columns] = s.astype(BF16)
        return carry

    lax.fori_loop(0, factor0.shape[1] // STEP, factors0, 0)
    back_to_twin(1)
    field[...] = jnp.zeros(field.shape, BF16)
    for pair in range(STRIPS // 2):
        columns = slice(pair * 2 * LANES, (pair + 1) * 2 * LANES)
        fr, fi = window(0, probe_row, reach, pair)
        r, i = incident[:reach, columns], incident[reach:, columns]
        field[:reach, columns] = (r * fr - i * fi).astype(BF16)
        field[BLOCK_IN : BLOCK_IN + reach, columns] = (r * fi + i * fr).astype(BF16)

    for copy in twin_copies[1]:
        copy.wait_recv()

    def factors1(step, carry):
        start = pl.multiple_of(step * STEP, 16)
        for strip in range(STRIPS):
            columns = slice(strip * LANES, (strip + 1) * LANES)
            values = kept[1, strip, pl.ds(start, STEP + 16), :].astype(F32)[RAD : RAD + STEP]
            c, s = cos_sin(values)
            factor1[0, pl.ds(start, STEP), columns] = c.astype(BF16)
            factor1[1, pl.ds(start, STEP), columns] = s.astype(BF16)
        return carry

    lax.fori_loop(0, factor1.shape[1] // STEP, factors1, 0)
    for load in loads[STRIPS:]:
        load.wait()

    def turned(mixed, count, beam, block):
        real, imag = mixed[:count], mixed[count:]
        pc = phase[beam, 0, pl.ds(block, 1), :]
        ps = phase[beam, 1, pl.ds(block, 1), :]
        return split(real * pc - imag * ps, real * ps + imag * pc)

    def pass_on(quarters, start, count):
        for q, (real, imag) in enumerate(quarters):
            columns = slice(q * QUARTER, (q + 1) * QUARTER)
            fr = factor1[0, pl.ds(start, count), columns].astype(F32)
            fi = factor1[1, pl.ds(start, count), columns].astype(F32)
            for beam in range(2):
                r, i = real[beam * count : (beam + 1) * count], imag[beam * count : (beam + 1) * count]
                passed[beam, 0, pl.ds(start, count), columns] = (r * fr - i * fi).astype(BF16)
                passed[beam, 1, pl.ds(start, count), columns] = (r * fi + i * fr).astype(BF16)

    def store(n, start, count):
        part = pl.ds(start, count)
        return pltpu.make_async_copy(
            passed.at[:, :, part], passed_out.at[:, :, part], store_sem.at[n]
        )

    def block_of(start):
        return jnp.concatenate(
            [factor0[0, pl.ds(start, BLOCK_IN), :], factor0[1, pl.ds(start, BLOCK_IN), :]], axis=0
        )

    def first_block(block, carry):
        start = pl.multiple_of(block * BLOCK, 16)
        mixed = dot(beam_taps[...], block_of(start))
        parts = [
            turned(mixed[2 * BLOCK * beam : 2 * BLOCK * (beam + 1)], BLOCK, beam, block)
            for beam in range(2)
        ]
        pass_on(propagate(parts, rings), start, BLOCK)
        store(block, start, BLOCK).start()
        return carry

    lax.fori_loop(0, FULL_BLOCKS, first_block, 0, unroll=2)

    out = PASSED - TAIL
    tops = [BLOCK * n for n in range(4)]
    left = jnp.concatenate([beam_taps[top : top + out] for top in tops])
    mixed = dot(left, block_of(TAIL))
    parts = [
        turned(mixed[2 * out * beam : 2 * out * (beam + 1)], out, beam, FULL_BLOCKS)
        for beam in range(2)
    ]
    mixed = dot(jnp.concatenate([taps[:out], taps[BLOCK : BLOCK + out]]), field[...])
    parts.append(split(mixed[:out], mixed[out:]))
    quarters = propagate(parts, rings)
    pass_on(quarters, TAIL, out)
    last = store(FULL_BLOCKS, TAIL, out)
    last.start()
    field[...] = jnp.zeros(field.shape, BF16)
    for pair in range(STRIPS // 2):
        columns = slice(pair * 2 * LANES, (pair + 1) * 2 * LANES)
        r, i = [
            jnp.concatenate([quarters[2 * pair + n][part][2 * out :] for n in range(2)], axis=1)
            for part in range(2)
        ]
        fr, fi = window(1, probe_row + RAD, out, pair)
        field[:out, columns] = (r * fr - i * fi).astype(BF16)
        field[BLOCK_IN : BLOCK_IN + out, columns] = (r * fi + i * fr).astype(BF16)
    field_copy = pltpu.make_async_copy(field, field_out, store_sem.at[FULL_BLOCKS + 1])
    field_copy.start()

    for copy in started:
        copy.wait_send()
    for s in range(2):
        for k in range(3):
            line_copy(s, k, whole, strip).wait_send()
        for n in range(2):

            @pl.when(place2 == edges[n][0])
            def _(s=s, n=n):
                for copy in edge_copies(s, n) + edge_spread(s, n):
                    copy.wait_send()

    for n in range(FULL_BLOCKS):
        store(n, n * BLOCK, BLOCK).wait()
    last.wait()
    field_copy.wait()


def first_slice(owners, tilts, amplitude, angle, positions, offsets, tiles):
    real, imag = row_matrices()
    taps = np.block([[real, -imag], [imag, real]]).astype(ml_dtypes.bfloat16)
    half = STRIPS // 2
    rows = tiles.shape[1]
    piece = rows // 4
    vmem = pl.BlockSpec(memory_space=pltpu.VMEM)
    smem = pl.BlockSpec(memory_space=pltpu.SMEM)
    anywhere = pl.BlockSpec(memory_space=pl.ANY)
    reach = BLOCK_IN - 4 * RAD
    return pl.pallas_call(
        first_kernel,
        out_shape=(
            jax.ShapeDtypeStruct((2, 2, PASSED, NPIX), BF16),
            jax.ShapeDtypeStruct((2 * BLOCK_IN, NPIX), BF16),
        ),
        in_specs=[smem] * 6 + [anywhere] + [vmem] * 2 + [anywhere] * 2,
        out_specs=(anywhere, anywhere),
        scratch_shapes=[
            pltpu.VMEM((lax.axis_size("beam"), 1, LANES), F32),
            pltpu.VMEM((half, rows, LANES), BF16),
            pltpu.VMEM((half, rows, LANES), BF16),
            pltpu.VMEM((half, rows, LANES), BF16),
            pltpu.VMEM((2, half, rows, LANES), BF16),
            pltpu.VMEM((2, 3, rows, LANES), BF16),
            pltpu.VMEM((2, rows, LANES), BF16),
            pltpu.VMEM((2, 3, piece, LANES), BF16),
            pltpu.VMEM((2, piece, LANES), BF16),
            pltpu.VMEM((2, piece, LANES), BF16),
            pltpu.VMEM((2, 2, AFTER, LANES), BF16),
            pltpu.VMEM((2, 2, BEFORE, LANES), BF16),
            pltpu.VMEM((2, STRIPS, KEPT, LANES), BF16),
            pltpu.VMEM((2 * BLOCK, 2 * BLOCK_IN), BF16),
            pltpu.VMEM((RINGS, 2 * QUARTER, 2 * QUARTER), BF16),
            pltpu.VMEM((2, TAIL + BLOCK_IN, NPIX), BF16),
            pltpu.VMEM((2, PASSED, NPIX), BF16),
            pltpu.VMEM((4 * BLOCK, 2 * BLOCK_IN), BF16),
            pltpu.VMEM((2, 2, 8, NPIX), F32),
            pltpu.VMEM((2 * reach, NPIX), F32),
            pltpu.VMEM((2 * BLOCK_IN, NPIX), BF16),
            pltpu.VMEM((2, 2, PASSED, NPIX), BF16),
            pltpu.SemaphoreType.DMA((STRIPS + 2,)),
            pltpu.SemaphoreType.DMA((half,)),
            pltpu.SemaphoreType.DMA((half,)),
            pltpu.SemaphoreType.DMA((2, 13)),
            pltpu.SemaphoreType.DMA((2, 13)),
            pltpu.SemaphoreType.DMA((2, 4)),
            pltpu.SemaphoreType.DMA((2, 4)),
            pltpu.SemaphoreType.DMA((2, 2, 5)),
            pltpu.SemaphoreType.DMA((2, 2, 3)),
            pltpu.SemaphoreType.DMA((8,)),
            pltpu.SemaphoreType.DMA((8,)),
            pltpu.SemaphoreType.DMA((FULL_BLOCKS + 2,)),
        ],
        compiler_params=pltpu.CompilerParams(
            collective_id=0, has_side_effects=True, vmem_limit_bytes=60 * 2**20
        ),
        name="first_slice",
    )(
        owners,
        tilts,
        amplitude,
        angle,
        positions,
        offsets,
        tiles,
        jnp.asarray(real),
        jnp.asarray(imag),
        jnp.asarray(taps),
        jnp.asarray(ring_matrices()),
    )


def second_kernel(
    positions,
    taps_held,
    rings_held,
    passed_in,
    field_in,
    exit_out,
    probe,
    taps,
    rings,
    field,
    passed,
    waves,
    load_sem,
    store_sem,
):
    probe_id = lax.axis_index("row") * lax.axis_size("beam") + lax.axis_index("beam")
    loads, others = [], []
    end = 0
    for n in range(FULL_BLOCKS + 1):
        start, end = end, min(n * BLOCK + BLOCK_IN, PASSED)
        loads.append(
            pltpu.make_async_copy(
                passed_in.at[:, :, start:end], passed.at[:, :, start:end], load_sem.at[n]
            )
        )
        loads[n].start()
        if n == 0:
            for m, pair in enumerate(((taps_held, taps), (rings_held, rings), (field_in, field))):
                others.append(pltpu.make_async_copy(*pair, load_sem.at[FULL_BLOCKS + 1 + m]))
                others[m].start()
    spare = passed.shape[2] - PASSED
    passed[:, :, PASSED:, :] = jnp.zeros((2, 2, spare, NPIX), BF16)

    def block_of(beam, start):
        return jnp.concatenate(
            [passed[beam, 0, start : start + BLOCK_IN], passed[beam, 1, start : start + BLOCK_IN]],
            axis=0,
        )

    stores = []

    def write(quarters, start, count):
        for q, (real, imag) in enumerate(quarters):
            for beam in range(2):
                chosen = slice(beam * count, (beam + 1) * count)
                low = q * QUARTER
                waves[beam, start : start + count, low : low + QUARTER] = real[chosen].astype(BF16)
                low += NPIX
                waves[beam, start : start + count, low : low + QUARTER] = imag[chosen].astype(BF16)
        part = slice(start, start + count)
        stores.append(
            pltpu.make_async_copy(
                waves.at[:, part], exit_out.at[:, part], store_sem.at[len(stores)]
            )
        )
        stores[-1].start()

    others[0].wait()
    for block in range(FULL_BLOCKS):
        loads[block].wait()
        start = block * BLOCK
        parts = []
        for beam in range(2):
            mixed = dot(taps[...], block_of(beam, start))
            parts.append(split(mixed[:BLOCK], mixed[BLOCK:]))
        if block == 0:
            others[1].wait()
        write(propagate(parts, rings), start, BLOCK)

    loads[FULL_BLOCKS].wait()
    others[2].wait()
    left = jnp.concatenate([taps[:WIN], taps[BLOCK : BLOCK + WIN]])
    parts = []
    for mixed in [dot(left, block_of(beam, TAIL)) for beam in range(2)] + [dot(left, field[...])]:
        parts.append(split(mixed[:WIN], mixed[WIN:]))
    quarters = propagate(parts, rings)
    write(quarters, TAIL, WIN)
    shift = (NPIX - positions[1, probe_id]) & (NPIX - 1)
    real = jnp.concatenate([real[2 * WIN :] for real, _ in quarters], axis=1)
    imag = jnp.concatenate([imag[2 * WIN :] for _, imag in quarters], axis=1)
    real = pltpu.roll(real, shift, 1)[:, :WIN]
    imag = pltpu.roll(imag, shift, 1)[:, :WIN]
    probe[0, 0] = jnp.concatenate([real, imag], axis=1)
    for copy in stores:
        copy.wait()


def second_slice(positions, passed, field):
    real, imag = row_matrices()
    taps = np.block([[real, -imag], [imag, real]]).astype(ml_dtypes.bfloat16)
    vmem = pl.BlockSpec(memory_space=pltpu.VMEM)
    smem = pl.BlockSpec(memory_space=pltpu.SMEM)
    anywhere = pl.BlockSpec(memory_space=pl.ANY)
    return pl.pallas_call(
        second_kernel,
        out_shape=(
            jax.ShapeDtypeStruct((2, NPIX // 2, 2 * NPIX), BF16),
            jax.ShapeDtypeStruct((1, 1, WIN, 2 * WIN), F32),
        ),
        in_specs=[smem] + [anywhere] * 4,
        out_specs=(anywhere, vmem),
        scratch_shapes=[
            pltpu.VMEM((2 * BLOCK, 2 * BLOCK_IN), BF16),
            pltpu.VMEM((RINGS, 2 * QUARTER, 2 * QUARTER), BF16),
            pltpu.VMEM((2 * BLOCK_IN, NPIX), BF16),
            pltpu.VMEM((2, 2, TAIL + BLOCK_IN, NPIX), BF16),
            pltpu.VMEM((2, NPIX // 2, 2 * NPIX), BF16),
            pltpu.SemaphoreType.DMA((FULL_BLOCKS + 4,)),
            pltpu.SemaphoreType.DMA((FULL_BLOCKS + 1,)),
        ],
        compiler_params=pltpu.CompilerParams(vmem_limit_bytes=60 * 2**20),
        name="second_slice",
    )(positions, jnp.asarray(taps), jnp.asarray(ring_matrices()), passed, field)


def body(tilts, potentials, owners, beam_amplitude, beam_phase, probe_positions, beam_offsets):
    positions = probe_positions.T
    passed, field = first_slice(
        owners, tilts, beam_amplitude, beam_phase, positions, beam_offsets, potentials
    )
    return second_slice(positions, passed, field)


def solution(mesh):
    return jax.shard_map(
        body,
        mesh=mesh,
        in_specs=(P("beam", None), P("beam", "row", None), P(), P("beam"), P("beam"), P(), P()),
        out_specs=(P("beam", "row", None), P("row", "beam", None, None)),
        check_vma=False,
    )
```

```python
import math

import jax
import jax.numpy as jnp
import ml_dtypes
import numpy as np
from jax import lax
from jax.experimental import pallas as pl
from jax.experimental.pallas import tpu as pltpu
from jax.sharding import PartitionSpec as P

NPIX = 1024
RAD = 8
WIN = 64
ROW_CHIRP = 0.07
RINGS = 8
QUARTER = NPIX // RINGS
LANES = 128
STRIPS = NPIX // LANES
BEFORE = 2 * RAD
AFTER = 80
KEPT = BEFORE + NPIX // 2 + AFTER
BLOCK_IN = 128
BLOCK = BLOCK_IN - 2 * RAD
FULL_BLOCKS = 4
TAIL = FULL_BLOCKS * BLOCK
PASSED = TAIL + BLOCK_IN - 6 * RAD
STEP = 48
F32 = jnp.float32
BF16 = jnp.bfloat16
MESH = pl.DeviceIdType.MESH


def row_taps():
    distance = np.arange(-RAD, RAD + 1) * 1.0
    envelope = np.exp(-0.5 * (distance / RAD) ** 2)
    angles = math.pi * ROW_CHIRP * distance**2
    norm = np.sqrt(np.sum(envelope**2))
    return envelope * np.cos(angles) / norm, envelope * np.sin(angles) / norm


def row_matrices():
    taps_real, taps_imag = row_taps()
    real = np.zeros((BLOCK, BLOCK_IN))
    imag = np.zeros((BLOCK, BLOCK_IN))
    for out in range(BLOCK):
        for position in range(2 * RAD + 1):
            offset = position - RAD
            real[out, out + RAD - offset] = taps_real[position]
            imag[out, out + RAD - offset] = taps_imag[position]
    return real.astype(np.float32), imag.astype(np.float32)


def ring_matrices():
    frequency = np.arange(NPIX) - NPIX // 2
    passband = (np.abs(frequency) * 3 <= NPIX) * 1.0
    phases = -6.0 * math.pi * (3.0 * frequency / NPIX) ** 2
    turns = np.mod(frequency[:, None] * np.arange(NPIX)[None, :], NPIX) * (2.0 * math.pi / NPIX)
    spectrum = passband * np.exp(1j * phases)
    kernel = (spectrum @ np.exp(1j * turns)) / NPIX
    held_real = kernel.real.astype(np.float32).astype(ml_dtypes.bfloat16).astype(np.float64)
    held_imag = kernel.imag.astype(np.float32).astype(ml_dtypes.bfloat16).astype(np.float64)
    quarters = (held_real + 1j * held_imag).reshape(RINGS, QUARTER)
    steps = np.arange(QUARTER)[None, :] - np.arange(QUARTER)[:, None]
    matrices = []
    for ring in range(RINGS):
        root = np.exp(2j * np.pi * ring / RINGS)
        folded = sum(root**part * quarters[part] for part in range(RINGS)) / RINGS
        matrix = np.where(steps >= 0, 1.0, root) * folded[steps % QUARTER]
        matrices.append(
            np.block([[matrix.real, matrix.imag], [-matrix.imag, matrix.real]]).astype(np.float32)
        )
    return np.stack(matrices).astype(ml_dtypes.bfloat16)


def fitted(function, degree, reach=1.0):
    nodes = reach * np.cos(np.pi * (np.arange(64) + 0.5) / 64)
    powers = np.stack([nodes**power for power in degree], axis=1)
    return [float(c) for c in np.linalg.lstsq(powers, function(nodes), rcond=None)[0]]


def polynomial(coefficients, square):
    total = coefficients[-1]
    for c in coefficients[-2::-1]:
        total = total * square + c
    return total


EVEN = fitted(np.cos, (0, 2, 4, 6))
ODD = fitted(np.sin, (1, 3, 5, 7))
TURN_EVEN = fitted(lambda u: np.cos(2 * np.pi * u), range(0, 17, 2), 0.5)
TURN_ODD = fitted(lambda u: np.sin(2 * np.pi * u), range(1, 18, 2), 0.5)


def circle(turns):
    square = turns * turns
    return polynomial(TURN_EVEN, square), polynomial(TURN_ODD, square) * turns


def phasor(steps):
    return circle((((steps + NPIX // 2) & (NPIX - 1)) - NPIX // 2).astype(F32) * (1.0 / NPIX))


def cos_sin(values):
    shifted = values - 1.0
    square = shifted * shifted
    even = polynomial(EVEN, square)
    odd = polynomial(ODD, square) * shifted
    c1, s1 = math.cos(1.0), math.sin(1.0)
    return c1 * even - s1 * odd, s1 * even + c1 * odd


def dot(a, b):
    return jnp.dot(a, b, preferred_element_type=F32)


HALF = math.sqrt(0.5)


def add(a, b):
    return a[0] + b[0], a[1] + b[1]


def less(a, b):
    return a[0] - b[0], a[1] - b[1]


def plus_i(a, b):
    return a[0] - b[1], a[1] + b[0]


def less_i(a, b):
    return a[0] + b[1], a[1] - b[0]


def split(real, imag):
    x = [
        tuple(f[:, q * QUARTER : (q + 1) * QUARTER] for f in (real, imag)) for q in range(RINGS)
    ]
    rings = [None] * RINGS
    for odd in range(2):
        a = [(less if odd else add)(x[q], x[q + 4]) for q in range(4)]
        if odd:
            a[1] = ((a[1][0] - a[1][1]) * HALF, (a[1][0] + a[1][1]) * HALF)
            a[3] = ((a[3][0] + a[3][1]) * -HALF, (a[3][0] - a[3][1]) * HALF)
            b, c = plus_i(a[0], a[2]), add(a[1], a[3])
            e, d = less_i(a[0], a[2]), less(a[1], a[3])
        else:
            b, c = add(a[0], a[2]), add(a[1], a[3])
            e, d = less(a[0], a[2]), less(a[1], a[3])
        rings[odd], rings[4 + odd] = add(b, c), less(b, c)
        rings[2 + odd], rings[6 + odd] = plus_i(e, d), less_i(e, d)
    return [jnp.concatenate([p.astype(BF16), q.astype(BF16)], axis=1) for p, q in rings]


def join(products):
    y = [(p[:, :QUARTER], p[:, QUARTER:]) for p in products]
    halves = []
    for odd in range(2):
        b, e = add(y[odd], y[4 + odd]), less(y[odd], y[4 + odd])
        c, d = add(y[2 + odd], y[6 + odd]), less(y[2 + odd], y[6 + odd])
        halves.append([add(b, c), less_i(e, d), less(b, c), plus_i(e, d)])
    even, o = halves
    o[1] = ((o[1][0] + o[1][1]) * HALF, (o[1][1] - o[1][0]) * HALF)
    o[3] = ((o[3][1] - o[3][0]) * HALF, (o[3][0] + o[3][1]) * -HALF)
    first = [add(even[0], o[0]), add(even[1], o[1]), less_i(even[2], o[2]), add(even[3], o[3])]
    last = [less(even[0], o[0]), less(even[1], o[1]), plus_i(even[2], o[2]), less(even[3], o[3])]
    return first + last


def propagate(parts, rings):
    return join([dot(jnp.concatenate(p, axis=0), rings[j]) for j, p in enumerate(zip(*parts))])


def first_kernel(
    owners_held,
    tilts_held,
    amplitude_held,
    angle_held,
    positions_held,
    offsets_held,
    tiles,
    taps_real_held,
    taps_imag_held,
    taps_held,
    rings_held,
    passed_out,
    field_out,
    owners,
    tilts,
    amplitude,
    angle,
    positions,
    offsets,
    taps_real,
    taps_imag,
    beams,
    own,
    other,
    sent,
    masked,
    arrived1,
    summed1,
    arrived2,
    summed2,
    arrived3,
    after_in,
    before_in,
    kept,
    taps,
    rings,
    factor0,
    factor1,
    beam_taps,
    phase,
    incident,
    field,
    passed,
    load_sem,
    swap_send,
    swap_recv,
    send_sem,
    recv_sem,
    twin_send,
    twin_recv,
    edge_send,
    edge_recv,
    beam_send,
    beam_recv,
    store_sem,
):
    me, block = lax.axis_index("beam"), lax.axis_index("row")
    core = me % 2
    x, y, z = me // 2 % 4, me // 8 % 4, me // 32
    half = STRIPS // 2
    rows = tiles.shape[1]
    piece = rows // 4
    probe_id = block * lax.axis_size("beam") + me
    row_start = block * rows

    def at(x, y, z, core):
        return ((z * 4 + y) * 4 + x) * 2 + core

    twin = at(x, y, z, 1 - core)
    facing = at(x, y, 1 - z, core)
    along_x = [at((x + k) % 4, y, z, core) for k in (1, 2, 3)]
    along_y = [at(x, (y + k) % 4, z, core) for k in (1, 2, 3)]
    place1 = x * (1 - core) + y * core
    place2 = y * (1 - core) + x * core
    line1 = [at((x + k * (1 - core)) % 4, (y + k * core) % 4, z, core) for k in (1, 2, 3)]
    line2 = [at((x + k * core) % 4, (y + k * (1 - core)) % 4, z, core) for k in (1, 2, 3)]

    barrier = pltpu.get_barrier_semaphore()
    partners = [(twin, block), (facing, block), (me, 1 - block), (facing, 1 - block)]
    partners += [(b, block) for b in along_x + along_y]
    for partner in partners:
        pl.semaphore_signal(barrier, inc=1, device_id=partner, device_id_type=MESH)

    held = (owners_held, tilts_held, amplitude_held, angle_held, positions_held, offsets_held)
    here = (owners, tilts, amplitude, angle, positions, offsets, taps_real, taps_imag)
    smalls = [
        pltpu.make_async_copy(a, b, load_sem.at[STRIPS + 2 + n])
        for n, (a, b) in enumerate(zip(held + (taps_real_held, taps_imag_held), here))
    ]
    for load in smalls:
        load.start()
    loads = []
    for group, target in enumerate((sent, own)):
        for strip in range(half):
            side = 1 - core if group == 0 else core
            column = pl.multiple_of((side * half + strip) * LANES, LANES)
            loads.append(
                pltpu.make_async_copy(
                    tiles.at[0, :, pl.ds(column, LANES)],
                    target.at[strip],
                    load_sem.at[group * half + strip],
                )
            )
    loads.append(pltpu.make_async_copy(rings_held, rings, load_sem.at[STRIPS]))
    loads.append(pltpu.make_async_copy(taps_held, taps, load_sem.at[STRIPS + 1]))
    for load in loads[:STRIPS]:
        load.start()

    for load in smalls:
        load.wait()
    probe_row = positions[0, probe_id] - row_start
    probe_column = positions[1, probe_id]

    lane = lax.broadcasted_iota(jnp.int32, (1, 1, LANES), 2)
    payload = jnp.zeros((1, 1, LANES), F32)
    for beam in range(2):
        values = (
            tilts[beam, 0].astype(F32),
            tilts[beam, 1].astype(F32),
            amplitude[beam],
            angle[beam],
        )
        for n, value in enumerate(values):
            payload = jnp.where(lane == 4 * beam + n, value, payload)
    beams[pl.ds(me, 1)] = payload

    for beam in range(2):
        tilt_row, tilt_column = tilts[beam, 0], tilts[beam, 1]
        pc, ps = phasor(tilt_row * lax.broadcasted_iota(jnp.int32, (8, BLOCK_IN), 1))
        pc, ps = pc[:1], ps[:1]
        real = taps_real[...] * pc - taps_imag[...] * ps
        imag = taps_real[...] * ps + taps_imag[...] * pc
        low = 2 * BLOCK * beam
        beam_taps[low : low + BLOCK, :] = jnp.concatenate([real, -imag], axis=1).astype(BF16)
        low += BLOCK
        beam_taps[low : low + BLOCK, :] = jnp.concatenate([imag, real], axis=1).astype(BF16)
        starts = row_start - BEFORE + BLOCK * lax.broadcasted_iota(jnp.int32, (8, NPIX), 0)
        pc, ps = phasor(
            tilt_row * starts + tilt_column * lax.broadcasted_iota(jnp.int32, (8, NPIX), 1)
        )
        phase[beam, 0] = pc
        phase[beam, 1] = ps

    pl.semaphore_wait(barrier, len(partners))
    started = []

    def copy_of(source, target, send_at, recv_at, device):
        return pltpu.make_async_remote_copy(
            src_ref=source,
            dst_ref=target,
            send_sem=send_at,
            recv_sem=recv_at,
            device_id=device,
            device_id_type=MESH,
        )

    def send(*args):
        copy = copy_of(*args)
        copy.start()
        started.append(copy)
        return copy

    def beam_chunk(size):
        return beams.at[pl.ds(pl.multiple_of(me // size * size, size), size)]

    chunk = beam_chunk(1)
    beam_copies = [send(chunk, chunk, beam_send.at[0], beam_recv.at[0], (twin, block))]
    swaps = []
    for strip in range(half):
        loads[strip].wait()
        swaps.append(
            send(
                sent.at[strip],
                other.at[strip],
                swap_send.at[strip],
                swap_recv.at[strip],
                (twin, block),
            )
        )
    for load in loads[half:STRIPS]:
        load.wait()
    for load in loads[STRIPS:]:
        load.start()

    def beam_step(size, devices, slot):
        for copy in beam_copies:
            copy.wait_recv()
        chunk = beam_chunk(size)
        beam_copies[:] = [
            send(chunk, chunk, beam_send.at[slot + k], beam_recv.at[slot + k], (device, block))
            for k, device in enumerate(devices)
        ]

    for swap in swaps:
        swap.wait_recv()

    copies = [None, None]

    def out_along_first(s):
        keep_own = jnp.where(owners[s] == me, 1.0, 0.0)
        keep_other = jnp.where(owners[s] == twin, 1.0, 0.0)
        for strip in range(half):
            value = own[strip].astype(F32) * keep_own + other[strip].astype(F32) * keep_other
            masked[s, strip] = value.astype(BF16)
        copies[s] = [
            send(
                masked.at[s, (place1 + k + 1) % 4],
                arrived1.at[s, k],
                send_sem.at[s, k],
                recv_sem.at[s, k],
                (line1[k], block),
            )
            for k in range(3)
        ]

    def out_along_second(s):
        for copy in copies[s]:
            copy.wait_recv()
        total = masked[s, place1].astype(F32)
        for k in range(3):
            total += arrived1[s, k].astype(F32)
        summed1[s] = total.astype(BF16)
        copies[s] = [
            send(
                summed1.at[s, pl.ds(pl.multiple_of((place2 + k + 1) % 4 * piece, piece), piece)],
                arrived2.at[s, k],
                send_sem.at[s, k + 3],
                recv_sem.at[s, k + 3],
                (line2[k], block),
            )
            for k in range(3)
        ]

    out_along_first(0)
    beam_step(2, along_x, 1)
    out_along_first(1)
    out_along_second(0)
    beam_step(8, along_y, 4)
    out_along_second(1)

    edge_to = [(me, 1 - block), (facing, 1 - block)]
    edges = [
        (0, pl.ds(0, AFTER), after_in, pl.ds(BEFORE + rows, AFTER)),
        (3, pl.ds(piece - BEFORE, BEFORE), before_in, pl.ds(0, BEFORE)),
    ]

    def edge_copies(s, n):
        _, source, target, _ = edges[n]
        return [
            copy_of(
                summed2.at[s, source],
                target.at[s, k],
                edge_send.at[s, n, k],
                edge_recv.at[s, n, k],
                edge_to[k],
            )
            for k in range(2)
        ]

    def edge_spread(s, n, peers=range(3)):
        place = kept.at[s, strip, edges[n][3]]
        return [
            copy_of(
                place, place, edge_send.at[s, n, k + 2], edge_recv.at[s, n, 2], (line2[k], block)
            )
            for k in peers
        ]

    mine = pl.ds(pl.multiple_of(place2 * piece, piece), piece)
    mine_kept = pl.ds(pl.multiple_of(place2 * piece + BEFORE, BEFORE), piece)
    strip = core * half + place1

    def out_to_facing(s):
        for copy in copies[s]:
            copy.wait_recv()
        total = summed1[s, mine].astype(F32)
        for k in range(3):
            total += arrived2[s, k].astype(F32)
        summed2[s] = total.astype(BF16)
        copies[s] = [
            send(
                summed2.at[s],
                arrived3.at[s],
                send_sem.at[s, 6],
                recv_sem.at[s, 6],
                (facing, block),
            )
        ]
        for n in range(2):

            @pl.when(place2 == edges[n][0])
            def _(n=n):
                for copy in edge_copies(s, n):
                    copy.start()

    def back_along_second(s):
        copies[s][0].wait_recv()
        kept[s, strip, mine_kept] = (
            summed2[s].astype(F32) + arrived3[s].astype(F32)
        ).astype(BF16)
        place = kept.at[s, strip, mine_kept]
        copies[s] = [
            send(place, place, send_sem.at[s, k + 7], recv_sem.at[s, k + 7], (line2[k], block))
            for k in range(3)
        ]
        for n in range(2):

            @pl.when(place2 == edges[n][0])
            def _(n=n):
                for copy in edge_copies(s, n):
                    copy.wait_recv()
                arrived = edges[n][2]
                total = arrived[s, 0].astype(F32) + arrived[s, 1].astype(F32)
                kept[s, strip, edges[n][3]] = total.astype(BF16)
                for copy in edge_spread(s, n):
                    copy.start()

        onward(s, mine_kept)

    def line_copy(s, k, held, at_strip):
        place = kept.at[s, at_strip, held]
        return copy_of(
            place, place, send_sem.at[s, k + 10], recv_sem.at[s, k + 10], (line1[k], block)
        )

    def onward(s, held):
        for k in range(3):
            line_copy(s, k, held, strip).start()

    def strip_to_twin(s, n, at_strip):
        place = kept.at[s, at_strip]
        twin_copies[s].append(
            send(place, place, twin_send.at[s, n], twin_recv.at[s, n], (twin, block))
        )

    twin_copies = [[], []]
    whole = pl.ds(0, KEPT)

    def back_along_first(s):
        for k in (0, 2, 1):
            copies[s][k].wait_recv()
            came = (place2 + 3 - k) % 4 * piece + BEFORE
            onward(s, pl.ds(pl.multiple_of(came, BEFORE), piece))
        for n in range(2):

            @pl.when(place2 != edges[n][0])
            def _(n=n):
                edge_spread(s, n, [0])[0].wait_recv()

            onward(s, edges[n][3])
        strip_to_twin(s, 3, strip)

    def back_to_twin(s):
        for k in (0, 2, 1):
            line_copy(s, k, whole, strip).wait_recv()
            strip_to_twin(s, k, core * half + (place1 + 3 - k) % 4)

    out_to_facing(0)
    beam_step(32, [facing], 7)
    out_to_facing(1)
    back_along_second(0)
    back_along_second(1)
    back_along_first(0)
    back_along_first(1)

    for copy in beam_copies:
        copy.wait_recv()
    reach = BLOCK_IN - 4 * RAD
    table = beams[...].reshape(beams.shape[0], LANES)
    both = jnp.concatenate([table[:, 0:4], table[:, 4:8]], axis=0)
    count = both.shape[0]
    ids = lax.broadcasted_iota(jnp.int32, (count, 1), 0)
    ids = jnp.where(ids < count // 2, 2 * ids, 2 * ids - count + 1)
    ky = both[:, 0:1].astype(jnp.int32)
    kx = both[:, 1:2].astype(jnp.int32)
    inside = (((ids - offsets[probe_id] + count) & (count - 1)) < count // 2).astype(F32)
    weight = both[:, 2:3] * inside * (1.0 / math.sqrt(count // 2))
    angle_c, angle_s = circle(both[:, 3:4] * (0.5 / math.pi))
    rel = lax.broadcasted_iota(jnp.int32, (count, LANES), 1) - BEFORE
    pc, ps = phasor(ky * rel - kx * probe_column)
    left_real = weight * (angle_c * pc - angle_s * ps)
    left_imag = weight * (angle_s * pc + angle_c * ps)
    left_real, left_imag = left_real.T[:reach], left_imag.T[:reach]
    left = jnp.concatenate(
        [
            jnp.concatenate([left_real, -left_imag], axis=1),
            jnp.concatenate([left_imag, left_real], axis=1),
        ],
        axis=0,
    )
    high = left.astype(BF16)
    left = jnp.concatenate([high, (left - high.astype(F32)).astype(BF16)], axis=0)
    pc, ps = phasor(kx * lax.broadcasted_iota(jnp.int32, (count, LANES), 1))
    qc, qs = phasor(kx * (LANES * lax.broadcasted_iota(jnp.int32, (count, STRIPS), 1)))
    for pair in range(STRIPS // 2):
        right = []
        for n in (2 * pair, 2 * pair + 1):
            c, s = qc[:, n : n + 1], qs[:, n : n + 1]
            right.append(jnp.concatenate([pc * c - ps * s, pc * s + ps * c], axis=0).astype(BF16))
        wave = dot(left, jnp.concatenate(right, axis=1))
        columns = slice(pair * 2 * LANES, (pair + 1) * 2 * LANES)
        incident[:, columns] = wave[: 2 * reach] + wave[2 * reach :]

    back_to_twin(0)

    def window(s, first, count, pair):
        chosen = lax.broadcasted_iota(jnp.int32, (count, KEPT), 0) + first
        chosen = (lax.broadcasted_iota(jnp.int32, (count, KEPT), 1) == chosen).astype(BF16)
        held = jnp.concatenate([kept[s, 2 * pair], kept[s, 2 * pair + 1]], axis=1)
        c, s = cos_sin(dot(chosen, held))
        return c.astype(BF16).astype(F32), s.astype(BF16).astype(F32)

    for copy in twin_copies[0]:
        copy.wait_recv()

    def factors0(step, carry):
        held = pl.ds(pl.multiple_of(step * STEP, 16), STEP)
        for strip in range(STRIPS):
            columns = slice(strip * LANES, (strip + 1) * LANES)
            c, s = cos_sin(kept[0, strip, held, :].astype(F32))
            factor0[0, held, columns] = c.astype(BF16)
            factor0[1, held, columns] = s.astype(BF16)
        return carry

    lax.fori_loop(0, factor0.shape[1] // STEP, factors0, 0)
    back_to_twin(1)
    field[...] = jnp.zeros(field.shape, BF16)
    for pair in range(STRIPS // 2):
        columns = slice(pair * 2 * LANES, (pair + 1) * 2 * LANES)
        fr, fi = window(0, probe_row, reach, pair)
        r, i = incident[:reach, columns], incident[reach:, columns]
        field[:reach, columns] = (r * fr - i * fi).astype(BF16)
        field[BLOCK_IN : BLOCK_IN + reach, columns] = (r * fi + i * fr).astype(BF16)

    for copy in twin_copies[1]:
        copy.wait_recv()

    def factors1(step, carry):
        start = pl.multiple_of(step * STEP, 16)
        for strip in range(STRIPS):
            columns = slice(strip * LANES, (strip + 1) * LANES)
            values = kept[1, strip, pl.ds(start, STEP + 16), :].astype(F32)[RAD : RAD + STEP]
            c, s = cos_sin(values)
            factor1[0, pl.ds(start, STEP), columns] = c.astype(BF16)
            factor1[1, pl.ds(start, STEP), columns] = s.astype(BF16)
        return carry

    lax.fori_loop(0, factor1.shape[1] // STEP, factors1, 0)
    for load in loads[STRIPS:]:
        load.wait()

    def turned(mixed, count, beam, block):
        real, imag = mixed[:count], mixed[count:]
        pc = phase[beam, 0, pl.ds(block, 1), :]
        ps = phase[beam, 1, pl.ds(block, 1), :]
        return split(real * pc - imag * ps, real * ps + imag * pc)

    def pass_on(quarters, start, count):
        for q, (real, imag) in enumerate(quarters):
            columns = slice(q * QUARTER, (q + 1) * QUARTER)
            fr = factor1[0, pl.ds(start, count), columns].astype(F32)
            fi = factor1[1, pl.ds(start, count), columns].astype(F32)
            for beam in range(2):
                r, i = real[beam * count : (beam + 1) * count], imag[beam * count : (beam + 1) * count]
                passed[beam, 0, pl.ds(start, count), columns] = (r * fr - i * fi).astype(BF16)
                passed[beam, 1, pl.ds(start, count), columns] = (r * fi + i * fr).astype(BF16)

    def store(n, start, count):
        part = pl.ds(start, count)
        return pltpu.make_async_copy(
            passed.at[:, :, part], passed_out.at[:, :, part], store_sem.at[n]
        )

    def block_of(start):
        return jnp.concatenate(
            [factor0[0, pl.ds(start, BLOCK_IN), :], factor0[1, pl.ds(start, BLOCK_IN), :]], axis=0
        )

    def first_block(block, carry):
        start = pl.multiple_of(block * BLOCK, 16)
        mixed = dot(beam_taps[...], block_of(start))
        parts = [
            turned(mixed[2 * BLOCK * beam : 2 * BLOCK * (beam + 1)], BLOCK, beam, block)
            for beam in range(2)
        ]
        pass_on(propagate(parts, rings), start, BLOCK)
        store(block, start, BLOCK).start()
        return carry

    lax.fori_loop(0, FULL_BLOCKS, first_block, 0, unroll=2)

    out = PASSED - TAIL
    tops = [BLOCK * n for n in range(4)]
    left = jnp.concatenate([beam_taps[top : top + out] for top in tops])
    mixed = dot(left, block_of(TAIL))
    parts = [
        turned(mixed[2 * out * beam : 2 * out * (beam + 1)], out, beam, FULL_BLOCKS)
        for beam in range(2)
    ]
    mixed = dot(jnp.concatenate([taps[:out], taps[BLOCK : BLOCK + out]]), field[...])
    parts.append(split(mixed[:out], mixed[out:]))
    quarters = propagate(parts, rings)
    pass_on(quarters, TAIL, out)
    last = store(FULL_BLOCKS, TAIL, out)
    last.start()
    field[...] = jnp.zeros(field.shape, BF16)
    for pair in range(STRIPS // 2):
        columns = slice(pair * 2 * LANES, (pair + 1) * 2 * LANES)
        r, i = [
            jnp.concatenate([quarters[2 * pair + n][part][2 * out :] for n in range(2)], axis=1)
            for part in range(2)
        ]
        fr, fi = window(1, probe_row + RAD, out, pair)
        field[:out, columns] = (r * fr - i * fi).astype(BF16)
        field[BLOCK_IN : BLOCK_IN + out, columns] = (r * fi + i * fr).astype(BF16)
    field_copy = pltpu.make_async_copy(field, field_out, store_sem.at[FULL_BLOCKS + 1])
    field_copy.start()

    for copy in started:
        copy.wait_send()
    for s in range(2):
        for k in range(3):
            line_copy(s, k, whole, strip).wait_send()
        for n in range(2):

            @pl.when(place2 == edges[n][0])
            def _(s=s, n=n):
                for copy in edge_copies(s, n) + edge_spread(s, n):
                    copy.wait_send()

    for n in range(FULL_BLOCKS):
        store(n, n * BLOCK, BLOCK).wait()
    last.wait()
    field_copy.wait()


def first_slice(owners, tilts, amplitude, angle, positions, offsets, tiles):
    real, imag = row_matrices()
    taps = np.block([[real, -imag], [imag, real]]).astype(ml_dtypes.bfloat16)
    half = STRIPS // 2
    rows = tiles.shape[1]
    piece = rows // 4
    anywhere = pl.BlockSpec(memory_space=pl.ANY)
    reach = BLOCK_IN - 4 * RAD
    return pl.pallas_call(
        first_kernel,
        out_shape=(
            jax.ShapeDtypeStruct((2, 2, PASSED, NPIX), BF16),
            jax.ShapeDtypeStruct((2 * BLOCK_IN, NPIX), BF16),
        ),
        in_specs=[anywhere] * 11,
        out_specs=(anywhere, anywhere),
        scratch_shapes=[
            pltpu.SMEM(owners.shape, owners.dtype),
            pltpu.SMEM(tilts.shape, tilts.dtype),
            pltpu.SMEM(amplitude.shape, amplitude.dtype),
            pltpu.SMEM(angle.shape, angle.dtype),
            pltpu.SMEM(positions.shape, positions.dtype),
            pltpu.SMEM(offsets.shape, offsets.dtype),
            pltpu.VMEM(real.shape, F32),
            pltpu.VMEM(real.shape, F32),
            pltpu.VMEM((lax.axis_size("beam"), 1, LANES), F32),
            pltpu.VMEM((half, rows, LANES), BF16),
            pltpu.VMEM((half, rows, LANES), BF16),
            pltpu.VMEM((half, rows, LANES), BF16),
            pltpu.VMEM((2, half, rows, LANES), BF16),
            pltpu.VMEM((2, 3, rows, LANES), BF16),
            pltpu.VMEM((2, rows, LANES), BF16),
            pltpu.VMEM((2, 3, piece, LANES), BF16),
            pltpu.VMEM((2, piece, LANES), BF16),
            pltpu.VMEM((2, piece, LANES), BF16),
            pltpu.VMEM((2, 2, AFTER, LANES), BF16),
            pltpu.VMEM((2, 2, BEFORE, LANES), BF16),
            pltpu.VMEM((2, STRIPS, KEPT, LANES), BF16),
            pltpu.VMEM((2 * BLOCK, 2 * BLOCK_IN), BF16),
            pltpu.VMEM((RINGS, 2 * QUARTER, 2 * QUARTER), BF16),
            pltpu.VMEM((2, TAIL + BLOCK_IN, NPIX), BF16),
            pltpu.VMEM((2, PASSED, NPIX), BF16),
            pltpu.VMEM((4 * BLOCK, 2 * BLOCK_IN), BF16),
            pltpu.VMEM((2, 2, 8, NPIX), F32),
            pltpu.VMEM((2 * reach, NPIX), F32),
            pltpu.VMEM((2 * BLOCK_IN, NPIX), BF16),
            pltpu.VMEM((2, 2, PASSED, NPIX), BF16),
            pltpu.SemaphoreType.DMA((STRIPS + 10,)),
            pltpu.SemaphoreType.DMA((half,)),
            pltpu.SemaphoreType.DMA((half,)),
            pltpu.SemaphoreType.DMA((2, 13)),
            pltpu.SemaphoreType.DMA((2, 13)),
            pltpu.SemaphoreType.DMA((2, 4)),
            pltpu.SemaphoreType.DMA((2, 4)),
            pltpu.SemaphoreType.DMA((2, 2, 5)),
            pltpu.SemaphoreType.DMA((2, 2, 3)),
            pltpu.SemaphoreType.DMA((8,)),
            pltpu.SemaphoreType.DMA((8,)),
            pltpu.SemaphoreType.DMA((FULL_BLOCKS + 2,)),
        ],
        compiler_params=pltpu.CompilerParams(
            collective_id=0, has_side_effects=True, vmem_limit_bytes=60 * 2**20
        ),
        name="first_slice",
    )(
        owners,
        tilts,
        amplitude,
        angle,
        positions,
        offsets,
        tiles,
        jnp.asarray(real),
        jnp.asarray(imag),
        jnp.asarray(taps),
        jnp.asarray(ring_matrices()),
    )


def second_kernel(
    positions_held,
    taps_held,
    rings_held,
    passed_in,
    field_in,
    exit_out,
    probe,
    positions,
    taps,
    rings,
    field,
    passed,
    waves,
    load_sem,
    store_sem,
):
    probe_id = lax.axis_index("row") * lax.axis_size("beam") + lax.axis_index("beam")
    pairs = (
        (taps_held, taps),
        (rings_held, rings),
        (field_in, field),
        (positions_held, positions),
    )
    loads, others = [], []
    end = 0
    for n in range(FULL_BLOCKS + 1):
        start, end = end, min(n * BLOCK + BLOCK_IN, PASSED)
        loads.append(
            pltpu.make_async_copy(
                passed_in.at[:, :, start:end], passed.at[:, :, start:end], load_sem.at[n]
            )
        )
        loads[n].start()
        if n == 0:
            for m, pair in enumerate(pairs):
                others.append(pltpu.make_async_copy(*pair, load_sem.at[FULL_BLOCKS + 1 + m]))
                others[m].start()
    spare = passed.shape[2] - PASSED
    passed[:, :, PASSED:, :] = jnp.zeros((2, 2, spare, NPIX), BF16)

    def block_of(beam, start):
        return jnp.concatenate(
            [passed[beam, 0, start : start + BLOCK_IN], passed[beam, 1, start : start + BLOCK_IN]],
            axis=0,
        )

    stores = []

    def write(quarters, start, count):
        for q, (real, imag) in enumerate(quarters):
            for beam in range(2):
                chosen = slice(beam * count, (beam + 1) * count)
                low = q * QUARTER
                waves[beam, start : start + count, low : low + QUARTER] = real[chosen].astype(BF16)
                low += NPIX
                waves[beam, start : start + count, low : low + QUARTER] = imag[chosen].astype(BF16)
        part = slice(start, start + count)
        stores.append(
            pltpu.make_async_copy(
                waves.at[:, part], exit_out.at[:, part], store_sem.at[len(stores)]
            )
        )
        stores[-1].start()

    others[0].wait()
    for block in range(FULL_BLOCKS):
        loads[block].wait()
        start = block * BLOCK
        parts = []
        for beam in range(2):
            mixed = dot(taps[...], block_of(beam, start))
            parts.append(split(mixed[:BLOCK], mixed[BLOCK:]))
        if block == 0:
            others[1].wait()
        write(propagate(parts, rings), start, BLOCK)

    loads[FULL_BLOCKS].wait()
    others[2].wait()
    others[3].wait()
    left = jnp.concatenate([taps[:WIN], taps[BLOCK : BLOCK + WIN]])
    parts = []
    for mixed in [dot(left, block_of(beam, TAIL)) for beam in range(2)] + [dot(left, field[...])]:
        parts.append(split(mixed[:WIN], mixed[WIN:]))
    quarters = propagate(parts, rings)
    write(quarters, TAIL, WIN)
    shift = (NPIX - positions[1, probe_id]) & (NPIX - 1)
    real = jnp.concatenate([real[2 * WIN :] for real, _ in quarters], axis=1)
    imag = jnp.concatenate([imag[2 * WIN :] for _, imag in quarters], axis=1)
    real = pltpu.roll(real, shift, 1)[:, :WIN]
    imag = pltpu.roll(imag, shift, 1)[:, :WIN]
    probe[0, 0] = jnp.concatenate([real, imag], axis=1)
    for copy in stores:
        copy.wait()


def second_slice(positions, passed, field):
    real, imag = row_matrices()
    taps = np.block([[real, -imag], [imag, real]]).astype(ml_dtypes.bfloat16)
    vmem = pl.BlockSpec(memory_space=pltpu.VMEM)
    anywhere = pl.BlockSpec(memory_space=pl.ANY)
    return pl.pallas_call(
        second_kernel,
        out_shape=(
            jax.ShapeDtypeStruct((2, NPIX // 2, 2 * NPIX), BF16),
            jax.ShapeDtypeStruct((1, 1, WIN, 2 * WIN), F32),
        ),
        in_specs=[anywhere] * 5,
        out_specs=(anywhere, vmem),
        scratch_shapes=[
            pltpu.SMEM(positions.shape, positions.dtype),
            pltpu.VMEM((2 * BLOCK, 2 * BLOCK_IN), BF16),
            pltpu.VMEM((RINGS, 2 * QUARTER, 2 * QUARTER), BF16),
            pltpu.VMEM((2 * BLOCK_IN, NPIX), BF16),
            pltpu.VMEM((2, 2, TAIL + BLOCK_IN, NPIX), BF16),
            pltpu.VMEM((2, NPIX // 2, 2 * NPIX), BF16),
            pltpu.SemaphoreType.DMA((FULL_BLOCKS + 5,)),
            pltpu.SemaphoreType.DMA((FULL_BLOCKS + 1,)),
        ],
        compiler_params=pltpu.CompilerParams(vmem_limit_bytes=60 * 2**20),
        name="second_slice",
    )(positions, jnp.asarray(taps), jnp.asarray(ring_matrices()), passed, field)


def body(tilts, potentials, owners, beam_amplitude, beam_phase, probe_positions, beam_offsets):
    positions = probe_positions.T
    passed, field = first_slice(
        owners, tilts, beam_amplitude, beam_phase, positions, beam_offsets, potentials
    )
    return second_slice(positions, passed, field)


def solution(mesh):
    return jax.shard_map(
        body,
        mesh=mesh,
        in_specs=(P("beam", None), P("beam", "row", None), P(), P("beam"), P("beam"), P(), P()),
        out_specs=(P("beam", "row", None), P("row", "beam", None, None)),
        check_vma=False,
    )
```

```python
import math

import jax
import jax.numpy as jnp
import ml_dtypes
import numpy as np
from jax import lax
from jax.experimental import pallas as pl
from jax.experimental.pallas import tpu as pltpu
from jax.sharding import PartitionSpec as P

NPIX = 1024
RAD = 8
WIN = 64
ROW_CHIRP = 0.07
RINGS = 8
QUARTER = NPIX // RINGS
LANES = 128
STRIPS = NPIX // LANES
BEFORE = 2 * RAD
AFTER = 80
KEPT = BEFORE + NPIX // 2 + AFTER
BLOCK_IN = 128
BLOCK = BLOCK_IN - 2 * RAD
FULL_BLOCKS = 4
TAIL = FULL_BLOCKS * BLOCK
PASSED = TAIL + BLOCK_IN - 6 * RAD
STEP = 48
F32 = jnp.float32
BF16 = jnp.bfloat16
MESH = pl.DeviceIdType.MESH


def row_taps():
    distance = np.arange(-RAD, RAD + 1) * 1.0
    envelope = np.exp(-0.5 * (distance / RAD) ** 2)
    angles = math.pi * ROW_CHIRP * distance**2
    norm = np.sqrt(np.sum(envelope**2))
    return envelope * np.cos(angles) / norm, envelope * np.sin(angles) / norm


def row_matrices():
    taps_real, taps_imag = row_taps()
    real = np.zeros((BLOCK, BLOCK_IN))
    imag = np.zeros((BLOCK, BLOCK_IN))
    for out in range(BLOCK):
        for position in range(2 * RAD + 1):
            offset = position - RAD
            real[out, out + RAD - offset] = taps_real[position]
            imag[out, out + RAD - offset] = taps_imag[position]
    return real.astype(np.float32), imag.astype(np.float32)


def ring_matrices():
    frequency = np.arange(NPIX) - NPIX // 2
    passband = (np.abs(frequency) * 3 <= NPIX) * 1.0
    phases = -6.0 * math.pi * (3.0 * frequency / NPIX) ** 2
    turns = np.mod(frequency[:, None] * np.arange(NPIX)[None, :], NPIX) * (2.0 * math.pi / NPIX)
    spectrum = passband * np.exp(1j * phases)
    kernel = (spectrum @ np.exp(1j * turns)) / NPIX
    held_real = kernel.real.astype(np.float32).astype(ml_dtypes.bfloat16).astype(np.float64)
    held_imag = kernel.imag.astype(np.float32).astype(ml_dtypes.bfloat16).astype(np.float64)
    quarters = (held_real + 1j * held_imag).reshape(RINGS, QUARTER)
    steps = np.arange(QUARTER)[None, :] - np.arange(QUARTER)[:, None]
    matrices = []
    for ring in range(RINGS):
        root = np.exp(2j * np.pi * ring / RINGS)
        folded = sum(root**part * quarters[part] for part in range(RINGS)) / RINGS
        matrix = np.where(steps >= 0, 1.0, root) * folded[steps % QUARTER]
        matrices.append(
            np.block([[matrix.real, matrix.imag], [-matrix.imag, matrix.real]]).astype(np.float32)
        )
    return np.stack(matrices).astype(ml_dtypes.bfloat16)


def fitted(function, degree, reach=1.0):
    nodes = reach * np.cos(np.pi * (np.arange(64) + 0.5) / 64)
    powers = np.stack([nodes**power for power in degree], axis=1)
    return [float(c) for c in np.linalg.lstsq(powers, function(nodes), rcond=None)[0]]


def polynomial(coefficients, square):
    total = coefficients[-1]
    for c in coefficients[-2::-1]:
        total = total * square + c
    return total


EVEN = fitted(np.cos, (0, 2, 4, 6))
ODD = fitted(np.sin, (1, 3, 5, 7))
TURN_EVEN = fitted(lambda u: np.cos(2 * np.pi * u), range(0, 17, 2), 0.5)
TURN_ODD = fitted(lambda u: np.sin(2 * np.pi * u), range(1, 18, 2), 0.5)


def circle(turns):
    square = turns * turns
    return polynomial(TURN_EVEN, square), polynomial(TURN_ODD, square) * turns


def phasor(steps):
    return circle((((steps + NPIX // 2) & (NPIX - 1)) - NPIX // 2).astype(F32) * (1.0 / NPIX))


def cos_sin(values):
    shifted = values - 1.0
    square = shifted * shifted
    even = polynomial(EVEN, square)
    odd = polynomial(ODD, square) * shifted
    c1, s1 = math.cos(1.0), math.sin(1.0)
    return c1 * even - s1 * odd, s1 * even + c1 * odd


def dot(a, b):
    return jnp.dot(a, b, preferred_element_type=F32)


HALF = math.sqrt(0.5)


def add(a, b):
    return a[0] + b[0], a[1] + b[1]


def less(a, b):
    return a[0] - b[0], a[1] - b[1]


def plus_i(a, b):
    return a[0] - b[1], a[1] + b[0]


def less_i(a, b):
    return a[0] + b[1], a[1] - b[0]


def split(real, imag):
    x = [
        tuple(f[:, q * QUARTER : (q + 1) * QUARTER] for f in (real, imag)) for q in range(RINGS)
    ]
    rings = [None] * RINGS
    for odd in range(2):
        a = [(less if odd else add)(x[q], x[q + 4]) for q in range(4)]
        if odd:
            a[1] = ((a[1][0] - a[1][1]) * HALF, (a[1][0] + a[1][1]) * HALF)
            a[3] = ((a[3][0] + a[3][1]) * -HALF, (a[3][0] - a[3][1]) * HALF)
            b, c = plus_i(a[0], a[2]), add(a[1], a[3])
            e, d = less_i(a[0], a[2]), less(a[1], a[3])
        else:
            b, c = add(a[0], a[2]), add(a[1], a[3])
            e, d = less(a[0], a[2]), less(a[1], a[3])
        rings[odd], rings[4 + odd] = add(b, c), less(b, c)
        rings[2 + odd], rings[6 + odd] = plus_i(e, d), less_i(e, d)
    return [jnp.concatenate([p.astype(BF16), q.astype(BF16)], axis=1) for p, q in rings]


def join(products):
    y = [(p[:, :QUARTER], p[:, QUARTER:]) for p in products]
    halves = []
    for odd in range(2):
        b, e = add(y[odd], y[4 + odd]), less(y[odd], y[4 + odd])
        c, d = add(y[2 + odd], y[6 + odd]), less(y[2 + odd], y[6 + odd])
        halves.append([add(b, c), less_i(e, d), less(b, c), plus_i(e, d)])
    even, o = halves
    o[1] = ((o[1][0] + o[1][1]) * HALF, (o[1][1] - o[1][0]) * HALF)
    o[3] = ((o[3][1] - o[3][0]) * HALF, (o[3][0] + o[3][1]) * -HALF)
    first = [add(even[0], o[0]), add(even[1], o[1]), less_i(even[2], o[2]), add(even[3], o[3])]
    last = [less(even[0], o[0]), less(even[1], o[1]), plus_i(even[2], o[2]), less(even[3], o[3])]
    return first + last


def propagate(parts, rings):
    return join([dot(jnp.concatenate(p, axis=0), rings[j]) for j, p in enumerate(zip(*parts))])


def first_kernel(
    owners_held,
    tilts_held,
    amplitude_held,
    angle_held,
    positions_held,
    offsets_held,
    tiles,
    taps_real_held,
    taps_imag_held,
    taps_held,
    rings_held,
    passed_out,
    field_out,
    owners,
    tilts,
    amplitude,
    angle,
    positions,
    offsets,
    taps_real,
    taps_imag,
    beams,
    own,
    other,
    sent,
    masked,
    arrived1,
    summed1,
    arrived2,
    summed2,
    arrived3,
    after_in,
    before_in,
    kept,
    taps,
    rings,
    factor0,
    factor1,
    beam_taps,
    phase,
    incident,
    field,
    passed,
    load_sem,
    swap_send,
    swap_recv,
    send_sem,
    recv_sem,
    twin_send,
    twin_recv,
    edge_send,
    edge_recv,
    beam_send,
    beam_recv,
    store_sem,
):
    me, block = lax.axis_index("beam"), lax.axis_index("row")
    core = me % 2
    x, y, z = me // 2 % 4, me // 8 % 4, me // 32
    half = STRIPS // 2
    rows = tiles.shape[1]
    piece = rows // 4
    probe_id = block * lax.axis_size("beam") + me
    row_start = block * rows

    def at(x, y, z, core):
        return ((z * 4 + y) * 4 + x) * 2 + core

    twin = at(x, y, z, 1 - core)
    facing = at(x, y, 1 - z, core)
    along_x = [at((x + k) % 4, y, z, core) for k in (1, 2, 3)]
    along_y = [at(x, (y + k) % 4, z, core) for k in (1, 2, 3)]
    place1 = x * (1 - core) + y * core
    place2 = y * (1 - core) + x * core
    line1 = [at((x + k * (1 - core)) % 4, (y + k * core) % 4, z, core) for k in (1, 2, 3)]
    line2 = [at((x + k * core) % 4, (y + k * (1 - core)) % 4, z, core) for k in (1, 2, 3)]

    barrier = pltpu.get_barrier_semaphore()
    partners = [(twin, block), (facing, block), (me, 1 - block), (facing, 1 - block)]
    partners += [(b, block) for b in along_x + along_y]
    for partner in partners:
        pl.semaphore_signal(barrier, inc=1, device_id=partner, device_id_type=MESH)

    held = (owners_held, tilts_held, amplitude_held, angle_held, positions_held, offsets_held)
    here = (owners, tilts, amplitude, angle, positions, offsets, taps_real, taps_imag)
    smalls = [
        pltpu.make_async_copy(a, b, load_sem.at[STRIPS + 2 + n])
        for n, (a, b) in enumerate(zip(held + (taps_real_held, taps_imag_held), here))
    ]
    for load in smalls:
        load.start()
    loads = []
    for group, target in enumerate((sent, own)):
        for strip in range(half):
            side = 1 - core if group == 0 else core
            column = pl.multiple_of((side * half + strip) * LANES, LANES)
            loads.append(
                pltpu.make_async_copy(
                    tiles.at[0, :, pl.ds(column, LANES)],
                    target.at[strip],
                    load_sem.at[group * half + strip],
                )
            )
    loads.append(pltpu.make_async_copy(rings_held, rings, load_sem.at[STRIPS]))
    loads.append(pltpu.make_async_copy(taps_held, taps, load_sem.at[STRIPS + 1]))
    for load in loads[:STRIPS]:
        load.start()

    for load in smalls:
        load.wait()
    probe_row = positions[0, probe_id] - row_start
    probe_column = positions[1, probe_id]

    lane = lax.broadcasted_iota(jnp.int32, (1, 1, LANES), 2)
    payload = jnp.zeros((1, 1, LANES), F32)
    for beam in range(2):
        values = (
            tilts[beam, 0].astype(F32),
            tilts[beam, 1].astype(F32),
            amplitude[beam],
            angle[beam],
        )
        for n, value in enumerate(values):
            payload = jnp.where(lane == 4 * beam + n, value, payload)
    beams[pl.ds(me, 1)] = payload

    for beam in range(2):
        tilt_row, tilt_column = tilts[beam, 0], tilts[beam, 1]
        pc, ps = phasor(tilt_row * lax.broadcasted_iota(jnp.int32, (8, BLOCK_IN), 1))
        pc, ps = pc[:1], ps[:1]
        real = taps_real[...] * pc - taps_imag[...] * ps
        imag = taps_real[...] * ps + taps_imag[...] * pc
        low = 2 * BLOCK * beam
        beam_taps[low : low + BLOCK, :] = jnp.concatenate([real, -imag], axis=1).astype(BF16)
        low += BLOCK
        beam_taps[low : low + BLOCK, :] = jnp.concatenate([imag, real], axis=1).astype(BF16)
        starts = row_start - BEFORE + BLOCK * lax.broadcasted_iota(jnp.int32, (8, NPIX), 0)
        pc, ps = phasor(
            tilt_row * starts + tilt_column * lax.broadcasted_iota(jnp.int32, (8, NPIX), 1)
        )
        phase[beam, 0] = pc
        phase[beam, 1] = ps

    pl.semaphore_wait(barrier, len(partners))
    started = []

    def copy_of(source, target, send_at, recv_at, device):
        return pltpu.make_async_remote_copy(
            src_ref=source,
            dst_ref=target,
            send_sem=send_at,
            recv_sem=recv_at,
            device_id=device,
            device_id_type=MESH,
        )

    def send(*args):
        copy = copy_of(*args)
        copy.start()
        started.append(copy)
        return copy

    def beam_chunk(size):
        return beams.at[pl.ds(pl.multiple_of(me // size * size, size), size)]

    chunk = beam_chunk(1)
    beam_copies = [send(chunk, chunk, beam_send.at[0], beam_recv.at[0], (twin, block))]
    swaps = []
    for strip in range(half):
        loads[strip].wait()
        swaps.append(
            send(
                sent.at[strip],
                other.at[strip],
                swap_send.at[strip],
                swap_recv.at[strip],
                (twin, block),
            )
        )
    for load in loads[half:STRIPS]:
        load.wait()
    for load in loads[STRIPS:]:
        load.start()

    def beam_step(size, devices, slot):
        for copy in beam_copies:
            copy.wait_recv()
        chunk = beam_chunk(size)
        beam_copies[:] = [
            send(chunk, chunk, beam_send.at[slot + k], beam_recv.at[slot + k], (device, block))
            for k, device in enumerate(devices)
        ]

    for swap in swaps:
        swap.wait_recv()

    copies = [None, None]

    def out_along_first(s):
        keep_own = jnp.where(owners[s] == me, 1.0, 0.0)
        keep_other = jnp.where(owners[s] == twin, 1.0, 0.0)
        for strip in range(half):
            value = own[strip].astype(F32) * keep_own + other[strip].astype(F32) * keep_other
            masked[s, strip] = value.astype(BF16)
        copies[s] = [
            send(
                masked.at[s, (place1 + k + 1) % 4],
                arrived1.at[s, k],
                send_sem.at[s, k],
                recv_sem.at[s, k],
                (line1[k], block),
            )
            for k in range(3)
        ]

    def out_along_second(s):
        for copy in copies[s]:
            copy.wait_recv()
        total = masked[s, place1].astype(F32)
        for k in range(3):
            total += arrived1[s, k].astype(F32)
        summed1[s] = total.astype(BF16)
        copies[s] = [
            send(
                summed1.at[s, pl.ds(pl.multiple_of((place2 + k + 1) % 4 * piece, piece), piece)],
                arrived2.at[s, k],
                send_sem.at[s, k + 3],
                recv_sem.at[s, k + 3],
                (line2[k], block),
            )
            for k in range(3)
        ]

    out_along_first(0)
    beam_step(2, along_x, 1)
    out_along_first(1)
    out_along_second(0)
    beam_step(8, along_y, 4)
    out_along_second(1)

    edge_to = [(me, 1 - block), (facing, 1 - block)]
    edges = [
        (0, pl.ds(0, AFTER), after_in, pl.ds(BEFORE + rows, AFTER)),
        (3, pl.ds(piece - BEFORE, BEFORE), before_in, pl.ds(0, BEFORE)),
    ]

    def edge_copies(s, n):
        _, source, target, _ = edges[n]
        return [
            copy_of(
                summed2.at[s, source],
                target.at[s, k],
                edge_send.at[s, n, k],
                edge_recv.at[s, n, k],
                edge_to[k],
            )
            for k in range(2)
        ]

    def edge_spread(s, n, peers=range(3)):
        place = kept.at[s, strip, edges[n][3]]
        return [
            copy_of(
                place, place, edge_send.at[s, n, k + 2], edge_recv.at[s, n, 2], (line2[k], block)
            )
            for k in peers
        ]

    mine = pl.ds(pl.multiple_of(place2 * piece, piece), piece)
    mine_kept = pl.ds(pl.multiple_of(place2 * piece + BEFORE, BEFORE), piece)
    strip = core * half + place1

    def out_to_facing(s):
        for copy in copies[s]:
            copy.wait_recv()
        total = summed1[s, mine].astype(F32)
        for k in range(3):
            total += arrived2[s, k].astype(F32)
        summed2[s] = total.astype(BF16)
        copies[s] = [
            send(
                summed2.at[s],
                arrived3.at[s],
                send_sem.at[s, 6],
                recv_sem.at[s, 6],
                (facing, block),
            )
        ]
        for n in range(2):

            @pl.when(place2 == edges[n][0])
            def _(n=n):
                for copy in edge_copies(s, n):
                    copy.start()

    def back_along_second(s):
        copies[s][0].wait_recv()
        kept[s, strip, mine_kept] = (
            summed2[s].astype(F32) + arrived3[s].astype(F32)
        ).astype(BF16)
        place = kept.at[s, strip, mine_kept]
        copies[s] = [
            send(place, place, send_sem.at[s, k + 7], recv_sem.at[s, k + 7], (line2[k], block))
            for k in range(3)
        ]
        for n in range(2):

            @pl.when(place2 == edges[n][0])
            def _(n=n):
                for copy in edge_copies(s, n):
                    copy.wait_recv()
                arrived = edges[n][2]
                total = arrived[s, 0].astype(F32) + arrived[s, 1].astype(F32)
                kept[s, strip, edges[n][3]] = total.astype(BF16)
                for copy in edge_spread(s, n):
                    copy.start()

        onward(s, mine_kept)

    def line_copy(s, k, held, at_strip):
        place = kept.at[s, at_strip, held]
        return copy_of(
            place, place, send_sem.at[s, k + 10], recv_sem.at[s, k + 10], (line1[k], block)
        )

    def onward(s, held):
        for k in range(3):
            line_copy(s, k, held, strip).start()

    def strip_to_twin(s, n, at_strip):
        place = kept.at[s, at_strip]
        twin_copies[s].append(
            send(place, place, twin_send.at[s, n], twin_recv.at[s, n], (twin, block))
        )

    twin_copies = [[], []]
    whole = pl.ds(0, KEPT)

    def back_along_first(s):
        for k in (0, 2, 1):
            copies[s][k].wait_recv()
            came = (place2 + 3 - k) % 4 * piece + BEFORE
            onward(s, pl.ds(pl.multiple_of(came, BEFORE), piece))
        for n in range(2):

            @pl.when(place2 != edges[n][0])
            def _(n=n):
                edge_spread(s, n, [0])[0].wait_recv()

            onward(s, edges[n][3])
        strip_to_twin(s, 3, strip)

    def back_to_twin(s):
        for k in (0, 2, 1):
            line_copy(s, k, whole, strip).wait_recv()
            strip_to_twin(s, k, core * half + (place1 + 3 - k) % 4)

    out_to_facing(0)
    beam_step(32, [facing], 7)
    out_to_facing(1)
    back_along_second(0)
    back_along_second(1)
    back_along_first(0)
    back_along_first(1)

    for copy in beam_copies:
        copy.wait_recv()
    reach = BLOCK_IN - 4 * RAD
    table = beams[...].reshape(beams.shape[0], LANES)
    both = jnp.concatenate([table[:, 0:4], table[:, 4:8]], axis=0)
    count = both.shape[0]
    ids = lax.broadcasted_iota(jnp.int32, (count, 1), 0)
    ids = jnp.where(ids < count // 2, 2 * ids, 2 * ids - count + 1)
    ky = both[:, 0:1].astype(jnp.int32)
    kx = both[:, 1:2].astype(jnp.int32)
    inside = (((ids - offsets[probe_id] + count) & (count - 1)) < count // 2).astype(F32)
    weight = both[:, 2:3] * inside * (1.0 / math.sqrt(count // 2))
    angle_c, angle_s = circle(both[:, 3:4] * (0.5 / math.pi))
    rel = lax.broadcasted_iota(jnp.int32, (count, LANES), 1) - BEFORE
    pc, ps = phasor(ky * rel - kx * probe_column)
    left_real = weight * (angle_c * pc - angle_s * ps)
    left_imag = weight * (angle_s * pc + angle_c * ps)
    left_real, left_imag = left_real.T[:reach], left_imag.T[:reach]
    left = jnp.concatenate(
        [
            jnp.concatenate([left_real, -left_imag], axis=1),
            jnp.concatenate([left_imag, left_real], axis=1),
        ],
        axis=0,
    )
    high = left.astype(BF16)
    left = jnp.concatenate([high, (left - high.astype(F32)).astype(BF16)], axis=0)
    pc, ps = phasor(kx * lax.broadcasted_iota(jnp.int32, (count, LANES), 1))
    qc, qs = phasor(kx * (LANES * lax.broadcasted_iota(jnp.int32, (count, STRIPS), 1)))
    for pair in range(STRIPS // 2):
        right = []
        for n in (2 * pair, 2 * pair + 1):
            c, s = qc[:, n : n + 1], qs[:, n : n + 1]
            right.append(jnp.concatenate([pc * c - ps * s, pc * s + ps * c], axis=0).astype(BF16))
        wave = dot(left, jnp.concatenate(right, axis=1))
        columns = slice(pair * 2 * LANES, (pair + 1) * 2 * LANES)
        incident[:, columns] = wave[: 2 * reach] + wave[2 * reach :]

    back_to_twin(0)

    def window(s, first, count, pair):
        chosen = lax.broadcasted_iota(jnp.int32, (count, KEPT), 0) + first
        chosen = (lax.broadcasted_iota(jnp.int32, (count, KEPT), 1) == chosen).astype(BF16)
        held = jnp.concatenate([kept[s, 2 * pair], kept[s, 2 * pair + 1]], axis=1)
        c, s = cos_sin(dot(chosen, held))
        return c.astype(BF16).astype(F32), s.astype(BF16).astype(F32)

    def factors0(side):
        def factors(step, carry):
            held = pl.ds(pl.multiple_of(step * STEP, 16), STEP)
            for n in range(half):
                at_strip = side * half + n
                columns = pl.ds(pl.multiple_of(at_strip * LANES, LANES), LANES)
                c, s = cos_sin(kept[0, at_strip, held, :].astype(F32))
                factor0[0, held, columns] = c.astype(BF16)
                factor0[1, held, columns] = s.astype(BF16)
            return carry

        lax.fori_loop(0, factor0.shape[1] // STEP, factors, 0)

    def probe_in(side):
        for n in range(half // 2):
            pair = side * (half // 2) + n
            columns = pl.ds(pl.multiple_of(pair * 2 * LANES, 2 * LANES), 2 * LANES)
            fr, fi = window(0, probe_row, reach, pair)
            r, i = incident[:reach, columns], incident[reach:, columns]
            field[:reach, columns] = (r * fr - i * fi).astype(BF16)
            field[BLOCK_IN : BLOCK_IN + reach, columns] = (r * fi + i * fr).astype(BF16)

    field[...] = jnp.zeros(field.shape, BF16)
    factors0(core)
    probe_in(core)
    for copy in twin_copies[0]:
        copy.wait_recv()
    factors0(1 - core)
    back_to_twin(1)

    def factors1(side):
        def factors(step, carry):
            start = pl.multiple_of(step * STEP, 16)
            for n in range(half):
                at_strip = side * half + n
                columns = pl.ds(pl.multiple_of(at_strip * LANES, LANES), LANES)
                values = kept[1, at_strip, pl.ds(start, STEP + 16), :].astype(F32)
                c, s = cos_sin(values[RAD : RAD + STEP])
                factor1[0, pl.ds(start, STEP), columns] = c.astype(BF16)
                factor1[1, pl.ds(start, STEP), columns] = s.astype(BF16)
            return carry

        lax.fori_loop(0, factor1.shape[1] // STEP, factors, 0)

    factors1(core)
    probe_in(1 - core)
    for copy in twin_copies[1]:
        copy.wait_recv()
    factors1(1 - core)
    for load in loads[STRIPS:]:
        load.wait()

    def turned(mixed, count, beam, block):
        real, imag = mixed[:count], mixed[count:]
        pc = phase[beam, 0, pl.ds(block, 1), :]
        ps = phase[beam, 1, pl.ds(block, 1), :]
        return split(real * pc - imag * ps, real * ps + imag * pc)

    def pass_on(quarters, start, count):
        for q, (real, imag) in enumerate(quarters):
            columns = slice(q * QUARTER, (q + 1) * QUARTER)
            fr = factor1[0, pl.ds(start, count), columns].astype(F32)
            fi = factor1[1, pl.ds(start, count), columns].astype(F32)
            for beam in range(2):
                r, i = real[beam * count : (beam + 1) * count], imag[beam * count : (beam + 1) * count]
                passed[beam, 0, pl.ds(start, count), columns] = (r * fr - i * fi).astype(BF16)
                passed[beam, 1, pl.ds(start, count), columns] = (r * fi + i * fr).astype(BF16)

    def store(n, start, count):
        part = pl.ds(start, count)
        return pltpu.make_async_copy(
            passed.at[:, :, part], passed_out.at[:, :, part], store_sem.at[n]
        )

    def block_of(start):
        return jnp.concatenate(
            [factor0[0, pl.ds(start, BLOCK_IN), :], factor0[1, pl.ds(start, BLOCK_IN), :]], axis=0
        )

    def first_block(block, carry):
        start = pl.multiple_of(block * BLOCK, 16)
        mixed = dot(beam_taps[...], block_of(start))
        parts = [
            turned(mixed[2 * BLOCK * beam : 2 * BLOCK * (beam + 1)], BLOCK, beam, block)
            for beam in range(2)
        ]
        pass_on(propagate(parts, rings), start, BLOCK)
        store(block, start, BLOCK).start()
        return carry

    lax.fori_loop(0, FULL_BLOCKS, first_block, 0, unroll=2)

    out = PASSED - TAIL
    tops = [BLOCK * n for n in range(4)]
    left = jnp.concatenate([beam_taps[top : top + out] for top in tops])
    mixed = dot(left, block_of(TAIL))
    parts = [
        turned(mixed[2 * out * beam : 2 * out * (beam + 1)], out, beam, FULL_BLOCKS)
        for beam in range(2)
    ]
    mixed = dot(jnp.concatenate([taps[:out], taps[BLOCK : BLOCK + out]]), field[...])
    parts.append(split(mixed[:out], mixed[out:]))
    quarters = propagate(parts, rings)
    pass_on(quarters, TAIL, out)
    last = store(FULL_BLOCKS, TAIL, out)
    last.start()
    field[...] = jnp.zeros(field.shape, BF16)
    for pair in range(STRIPS // 2):
        columns = slice(pair * 2 * LANES, (pair + 1) * 2 * LANES)
        r, i = [
            jnp.concatenate([quarters[2 * pair + n][part][2 * out :] for n in range(2)], axis=1)
            for part in range(2)
        ]
        fr, fi = window(1, probe_row + RAD, out, pair)
        field[:out, columns] = (r * fr - i * fi).astype(BF16)
        field[BLOCK_IN : BLOCK_IN + out, columns] = (r * fi + i * fr).astype(BF16)
    field_copy = pltpu.make_async_copy(field, field_out, store_sem.at[FULL_BLOCKS + 1])
    field_copy.start()

    for copy in started:
        copy.wait_send()
    for s in range(2):
        for k in range(3):
            line_copy(s, k, whole, strip).wait_send()
        for n in range(2):

            @pl.when(place2 == edges[n][0])
            def _(s=s, n=n):
                for copy in edge_copies(s, n) + edge_spread(s, n):
                    copy.wait_send()

    for n in range(FULL_BLOCKS):
        store(n, n * BLOCK, BLOCK).wait()
    last.wait()
    field_copy.wait()


def first_slice(owners, tilts, amplitude, angle, positions, offsets, tiles):
    real, imag = row_matrices()
    taps = np.block([[real, -imag], [imag, real]]).astype(ml_dtypes.bfloat16)
    half = STRIPS // 2
    rows = tiles.shape[1]
    piece = rows // 4
    anywhere = pl.BlockSpec(memory_space=pl.ANY)
    reach = BLOCK_IN - 4 * RAD
    return pl.pallas_call(
        first_kernel,
        out_shape=(
            jax.ShapeDtypeStruct((2, 2, PASSED, NPIX), BF16),
            jax.ShapeDtypeStruct((2 * BLOCK_IN, NPIX), BF16),
        ),
        in_specs=[anywhere] * 11,
        out_specs=(anywhere, anywhere),
        scratch_shapes=[
            pltpu.SMEM(owners.shape, owners.dtype),
            pltpu.SMEM(tilts.shape, tilts.dtype),
            pltpu.SMEM(amplitude.shape, amplitude.dtype),
            pltpu.SMEM(angle.shape, angle.dtype),
            pltpu.SMEM(positions.shape, positions.dtype),
            pltpu.SMEM(offsets.shape, offsets.dtype),
            pltpu.VMEM(real.shape, F32),
            pltpu.VMEM(real.shape, F32),
            pltpu.VMEM((lax.axis_size("beam"), 1, LANES), F32),
            pltpu.VMEM((half, rows, LANES), BF16),
            pltpu.VMEM((half, rows, LANES), BF16),
            pltpu.VMEM((half, rows, LANES), BF16),
            pltpu.VMEM((2, half, rows, LANES), BF16),
            pltpu.VMEM((2, 3, rows, LANES), BF16),
            pltpu.VMEM((2, rows, LANES), BF16),
            pltpu.VMEM((2, 3, piece, LANES), BF16),
            pltpu.VMEM((2, piece, LANES), BF16),
            pltpu.VMEM((2, piece, LANES), BF16),
            pltpu.VMEM((2, 2, AFTER, LANES), BF16),
            pltpu.VMEM((2, 2, BEFORE, LANES), BF16),
            pltpu.VMEM((2, STRIPS, KEPT, LANES), BF16),
            pltpu.VMEM((2 * BLOCK, 2 * BLOCK_IN), BF16),
            pltpu.VMEM((RINGS, 2 * QUARTER, 2 * QUARTER), BF16),
            pltpu.VMEM((2, TAIL + BLOCK_IN, NPIX), BF16),
            pltpu.VMEM((2, PASSED, NPIX), BF16),
            pltpu.VMEM((4 * BLOCK, 2 * BLOCK_IN), BF16),
            pltpu.VMEM((2, 2, 8, NPIX), F32),
            pltpu.VMEM((2 * reach, NPIX), F32),
            pltpu.VMEM((2 * BLOCK_IN, NPIX), BF16),
            pltpu.VMEM((2, 2, PASSED, NPIX), BF16),
            pltpu.SemaphoreType.DMA((STRIPS + 10,)),
            pltpu.SemaphoreType.DMA((half,)),
            pltpu.SemaphoreType.DMA((half,)),
            pltpu.SemaphoreType.DMA((2, 13)),
            pltpu.SemaphoreType.DMA((2, 13)),
            pltpu.SemaphoreType.DMA((2, 4)),
            pltpu.SemaphoreType.DMA((2, 4)),
            pltpu.SemaphoreType.DMA((2, 2, 5)),
            pltpu.SemaphoreType.DMA((2, 2, 3)),
            pltpu.SemaphoreType.DMA((8,)),
            pltpu.SemaphoreType.DMA((8,)),
            pltpu.SemaphoreType.DMA((FULL_BLOCKS + 2,)),
        ],
        compiler_params=pltpu.CompilerParams(
            collective_id=0, has_side_effects=True, vmem_limit_bytes=60 * 2**20
        ),
        name="first_slice",
    )(
        owners,
        tilts,
        amplitude,
        angle,
        positions,
        offsets,
        tiles,
        jnp.asarray(real),
        jnp.asarray(imag),
        jnp.asarray(taps),
        jnp.asarray(ring_matrices()),
    )


def second_kernel(
    positions_held,
    taps_held,
    rings_held,
    passed_in,
    field_in,
    exit_out,
    probe,
    positions,
    taps,
    rings,
    field,
    passed,
    waves,
    load_sem,
    store_sem,
):
    probe_id = lax.axis_index("row") * lax.axis_size("beam") + lax.axis_index("beam")
    pairs = (
        (taps_held, taps),
        (rings_held, rings),
        (field_in, field),
        (positions_held, positions),
    )
    loads, others = [], []
    end = 0
    for n in range(FULL_BLOCKS + 1):
        start, end = end, min(n * BLOCK + BLOCK_IN, PASSED)
        loads.append(
            pltpu.make_async_copy(
                passed_in.at[:, :, start:end], passed.at[:, :, start:end], load_sem.at[n]
            )
        )
        loads[n].start()
        if n == 0:
            for m, pair in enumerate(pairs):
                others.append(pltpu.make_async_copy(*pair, load_sem.at[FULL_BLOCKS + 1 + m]))
                others[m].start()
    spare = passed.shape[2] - PASSED
    passed[:, :, PASSED:, :] = jnp.zeros((2, 2, spare, NPIX), BF16)

    def block_of(beam, start):
        return jnp.concatenate(
            [passed[beam, 0, start : start + BLOCK_IN], passed[beam, 1, start : start + BLOCK_IN]],
            axis=0,
        )

    stores = []

    def write(quarters, start, count):
        for q, (real, imag) in enumerate(quarters):
            for beam in range(2):
                chosen = slice(beam * count, (beam + 1) * count)
                low = q * QUARTER
                waves[beam, start : start + count, low : low + QUARTER] = real[chosen].astype(BF16)
                low += NPIX
                waves[beam, start : start + count, low : low + QUARTER] = imag[chosen].astype(BF16)
        part = slice(start, start + count)
        stores.append(
            pltpu.make_async_copy(
                waves.at[:, part], exit_out.at[:, part], store_sem.at[len(stores)]
            )
        )
        stores[-1].start()

    others[0].wait()
    for block in range(FULL_BLOCKS):
        loads[block].wait()
        start = block * BLOCK
        parts = []
        for beam in range(2):
            mixed = dot(taps[...], block_of(beam, start))
            parts.append(split(mixed[:BLOCK], mixed[BLOCK:]))
        if block == 0:
            others[1].wait()
        write(propagate(parts, rings), start, BLOCK)

    loads[FULL_BLOCKS].wait()
    others[2].wait()
    others[3].wait()
    left = jnp.concatenate([taps[:WIN], taps[BLOCK : BLOCK + WIN]])
    parts = []
    for mixed in [dot(left, block_of(beam, TAIL)) for beam in range(2)] + [dot(left, field[...])]:
        parts.append(split(mixed[:WIN], mixed[WIN:]))
    quarters = propagate(parts, rings)
    write(quarters, TAIL, WIN)
    shift = (NPIX - positions[1, probe_id]) & (NPIX - 1)
    real = jnp.concatenate([real[2 * WIN :] for real, _ in quarters], axis=1)
    imag = jnp.concatenate([imag[2 * WIN :] for _, imag in quarters], axis=1)
    real = pltpu.roll(real, shift, 1)[:, :WIN]
    imag = pltpu.roll(imag, shift, 1)[:, :WIN]
    probe[0, 0] = jnp.concatenate([real, imag], axis=1)
    for copy in stores:
        copy.wait()


def second_slice(positions, passed, field):
    real, imag = row_matrices()
    taps = np.block([[real, -imag], [imag, real]]).astype(ml_dtypes.bfloat16)
    vmem = pl.BlockSpec(memory_space=pltpu.VMEM)
    anywhere = pl.BlockSpec(memory_space=pl.ANY)
    return pl.pallas_call(
        second_kernel,
        out_shape=(
            jax.ShapeDtypeStruct((2, NPIX // 2, 2 * NPIX), BF16),
            jax.ShapeDtypeStruct((1, 1, WIN, 2 * WIN), F32),
        ),
        in_specs=[anywhere] * 5,
        out_specs=(anywhere, vmem),
        scratch_shapes=[
            pltpu.SMEM(positions.shape, positions.dtype),
            pltpu.VMEM((2 * BLOCK, 2 * BLOCK_IN), BF16),
            pltpu.VMEM((RINGS, 2 * QUARTER, 2 * QUARTER), BF16),
            pltpu.VMEM((2 * BLOCK_IN, NPIX), BF16),
            pltpu.VMEM((2, 2, TAIL + BLOCK_IN, NPIX), BF16),
            pltpu.VMEM((2, NPIX // 2, 2 * NPIX), BF16),
            pltpu.SemaphoreType.DMA((FULL_BLOCKS + 5,)),
            pltpu.SemaphoreType.DMA((FULL_BLOCKS + 1,)),
        ],
        compiler_params=pltpu.CompilerParams(vmem_limit_bytes=60 * 2**20),
        name="second_slice",
    )(positions, jnp.asarray(taps), jnp.asarray(ring_matrices()), passed, field)


def body(tilts, potentials, owners, beam_amplitude, beam_phase, probe_positions, beam_offsets):
    positions = probe_positions.T
    passed, field = first_slice(
        owners, tilts, beam_amplitude, beam_phase, positions, beam_offsets, potentials
    )
    return second_slice(positions, passed, field)


def solution(mesh):
    return jax.shard_map(
        body,
        mesh=mesh,
        in_specs=(P("beam", None), P("beam", "row", None), P(), P("beam"), P("beam"), P(), P()),
        out_specs=(P("beam", "row", None), P("row", "beam", None, None)),
        check_vma=False,
    )
```

```python
import math

import jax
import jax.numpy as jnp
import ml_dtypes
import numpy as np
from jax import lax
from jax.experimental import pallas as pl
from jax.experimental.pallas import tpu as pltpu
from jax.sharding import PartitionSpec as P

NPIX = 1024
RAD = 8
WIN = 64
ROW_CHIRP = 0.07
RINGS = 8
QUARTER = NPIX // RINGS
LANES = 128
STRIPS = NPIX // LANES
BEFORE = 2 * RAD
AFTER = 80
KEPT = BEFORE + NPIX // 2 + AFTER
BLOCK_IN = 128
BLOCK = BLOCK_IN - 2 * RAD
FULL_BLOCKS = 4
TAIL = FULL_BLOCKS * BLOCK
PASSED = TAIL + BLOCK_IN - 6 * RAD
STEP = 48
F32 = jnp.float32
BF16 = jnp.bfloat16
MESH = pl.DeviceIdType.MESH


def row_taps():
    distance = np.arange(-RAD, RAD + 1) * 1.0
    envelope = np.exp(-0.5 * (distance / RAD) ** 2)
    angles = math.pi * ROW_CHIRP * distance**2
    norm = np.sqrt(np.sum(envelope**2))
    return envelope * np.cos(angles) / norm, envelope * np.sin(angles) / norm


def row_matrices():
    taps_real, taps_imag = row_taps()
    real = np.zeros((BLOCK, BLOCK_IN))
    imag = np.zeros((BLOCK, BLOCK_IN))
    for out in range(BLOCK):
        for position in range(2 * RAD + 1):
            offset = position - RAD
            real[out, out + RAD - offset] = taps_real[position]
            imag[out, out + RAD - offset] = taps_imag[position]
    return real.astype(np.float32), imag.astype(np.float32)


def ring_matrices():
    frequency = np.arange(NPIX) - NPIX // 2
    passband = (np.abs(frequency) * 3 <= NPIX) * 1.0
    phases = -6.0 * math.pi * (3.0 * frequency / NPIX) ** 2
    turns = np.mod(frequency[:, None] * np.arange(NPIX)[None, :], NPIX) * (2.0 * math.pi / NPIX)
    spectrum = passband * np.exp(1j * phases)
    kernel = (spectrum @ np.exp(1j * turns)) / NPIX
    held_real = kernel.real.astype(np.float32).astype(ml_dtypes.bfloat16).astype(np.float64)
    held_imag = kernel.imag.astype(np.float32).astype(ml_dtypes.bfloat16).astype(np.float64)
    quarters = (held_real + 1j * held_imag).reshape(RINGS, QUARTER)
    steps = np.arange(QUARTER)[None, :] - np.arange(QUARTER)[:, None]
    matrices = []
    for ring in range(RINGS):
        root = np.exp(2j * np.pi * ring / RINGS)
        folded = sum(root**part * quarters[part] for part in range(RINGS)) / RINGS
        matrix = np.where(steps >= 0, 1.0, root) * folded[steps % QUARTER]
        matrices.append(
            np.block([[matrix.real, matrix.imag], [-matrix.imag, matrix.real]]).astype(np.float32)
        )
    return np.stack(matrices).astype(ml_dtypes.bfloat16)


def fitted(function, degree, reach=1.0):
    nodes = reach * np.cos(np.pi * (np.arange(64) + 0.5) / 64)
    powers = np.stack([nodes**power for power in degree], axis=1)
    return [float(c) for c in np.linalg.lstsq(powers, function(nodes), rcond=None)[0]]


def polynomial(coefficients, square):
    total = coefficients[-1]
    for c in coefficients[-2::-1]:
        total = total * square + c
    return total


EVEN = fitted(np.cos, (0, 2, 4, 6))
ODD = fitted(np.sin, (1, 3, 5, 7))
TURN_EVEN = fitted(lambda u: np.cos(2 * np.pi * u), range(0, 17, 2), 0.5)
TURN_ODD = fitted(lambda u: np.sin(2 * np.pi * u), range(1, 18, 2), 0.5)


def circle(turns):
    square = turns * turns
    return polynomial(TURN_EVEN, square), polynomial(TURN_ODD, square) * turns


def phasor(steps):
    return circle((((steps + NPIX // 2) & (NPIX - 1)) - NPIX // 2).astype(F32) * (1.0 / NPIX))


def cos_sin(values):
    shifted = values - 1.0
    square = shifted * shifted
    even = polynomial(EVEN, square)
    odd = polynomial(ODD, square) * shifted
    c1, s1 = math.cos(1.0), math.sin(1.0)
    return c1 * even - s1 * odd, s1 * even + c1 * odd


def dot(a, b):
    return jnp.dot(a, b, preferred_element_type=F32)


HALF = math.sqrt(0.5)


def add(a, b):
    return a[0] + b[0], a[1] + b[1]


def less(a, b):
    return a[0] - b[0], a[1] - b[1]


def plus_i(a, b):
    return a[0] - b[1], a[1] + b[0]


def less_i(a, b):
    return a[0] + b[1], a[1] - b[0]


def split(real, imag):
    x = [
        tuple(f[:, q * QUARTER : (q + 1) * QUARTER] for f in (real, imag)) for q in range(RINGS)
    ]
    rings = [None] * RINGS
    for odd in range(2):
        a = [(less if odd else add)(x[q], x[q + 4]) for q in range(4)]
        if odd:
            a[1] = ((a[1][0] - a[1][1]) * HALF, (a[1][0] + a[1][1]) * HALF)
            a[3] = ((a[3][0] + a[3][1]) * -HALF, (a[3][0] - a[3][1]) * HALF)
            b, c = plus_i(a[0], a[2]), add(a[1], a[3])
            e, d = less_i(a[0], a[2]), less(a[1], a[3])
        else:
            b, c = add(a[0], a[2]), add(a[1], a[3])
            e, d = less(a[0], a[2]), less(a[1], a[3])
        rings[odd], rings[4 + odd] = add(b, c), less(b, c)
        rings[2 + odd], rings[6 + odd] = plus_i(e, d), less_i(e, d)
    return [jnp.concatenate([p.astype(BF16), q.astype(BF16)], axis=1) for p, q in rings]


def join(products):
    y = [(p[:, :QUARTER], p[:, QUARTER:]) for p in products]
    halves = []
    for odd in range(2):
        b, e = add(y[odd], y[4 + odd]), less(y[odd], y[4 + odd])
        c, d = add(y[2 + odd], y[6 + odd]), less(y[2 + odd], y[6 + odd])
        halves.append([add(b, c), less_i(e, d), less(b, c), plus_i(e, d)])
    even, o = halves
    o[1] = ((o[1][0] + o[1][1]) * HALF, (o[1][1] - o[1][0]) * HALF)
    o[3] = ((o[3][1] - o[3][0]) * HALF, (o[3][0] + o[3][1]) * -HALF)
    first = [add(even[0], o[0]), add(even[1], o[1]), less_i(even[2], o[2]), add(even[3], o[3])]
    last = [less(even[0], o[0]), less(even[1], o[1]), plus_i(even[2], o[2]), less(even[3], o[3])]
    return first + last


def propagate(parts, rings):
    return join([dot(jnp.concatenate(p, axis=0), rings[j]) for j, p in enumerate(zip(*parts))])


def first_kernel(
    owners_held,
    tilts_held,
    amplitude_held,
    angle_held,
    positions_held,
    offsets_held,
    tiles,
    taps_real_held,
    taps_imag_held,
    taps_held,
    rings_held,
    passed_out,
    field_out,
    owners,
    tilts,
    amplitude,
    angle,
    positions,
    offsets,
    taps_real,
    taps_imag,
    beams,
    own,
    other,
    masked,
    arrived1,
    summed1,
    arrived2,
    summed2,
    arrived3,
    after_in,
    before_in,
    kept,
    taps,
    rings,
    factor0,
    factor1,
    beam_taps,
    phase,
    incident,
    field,
    passed,
    load_sem,
    swap_send,
    swap_recv,
    send_sem,
    recv_sem,
    twin_send,
    twin_recv,
    edge_send,
    edge_recv,
    beam_send,
    beam_recv,
    store_sem,
):
    me, block = lax.axis_index("beam"), lax.axis_index("row")
    core = me % 2
    x, y, z = me // 2 % 4, me // 8 % 4, me // 32
    half = STRIPS // 2
    rows = tiles.shape[1]
    piece = rows // 4
    probe_id = block * lax.axis_size("beam") + me
    row_start = block * rows

    def at(x, y, z, core):
        return ((z * 4 + y) * 4 + x) * 2 + core

    twin = at(x, y, z, 1 - core)
    facing = at(x, y, 1 - z, core)
    along_x = [at((x + k) % 4, y, z, core) for k in (1, 2, 3)]
    along_y = [at(x, (y + k) % 4, z, core) for k in (1, 2, 3)]
    place1 = x * (1 - core) + y * core
    place2 = y * (1 - core) + x * core
    line1 = [at((x + k * (1 - core)) % 4, (y + k * core) % 4, z, core) for k in (1, 2, 3)]
    line2 = [at((x + k * core) % 4, (y + k * (1 - core)) % 4, z, core) for k in (1, 2, 3)]

    barrier = pltpu.get_barrier_semaphore()
    partners = [(twin, block), (facing, block), (me, 1 - block), (facing, 1 - block)]
    partners += [(b, block) for b in along_x + along_y]
    for partner in partners:
        pl.semaphore_signal(barrier, inc=1, device_id=partner, device_id_type=MESH)

    held = (owners_held, tilts_held, amplitude_held, angle_held, positions_held, offsets_held)
    here = (owners, tilts, amplitude, angle, positions, offsets, taps_real, taps_imag)
    smalls = [
        pltpu.make_async_copy(a, b, load_sem.at[STRIPS + 2 + n])
        for n, (a, b) in enumerate(zip(held + (taps_real_held, taps_imag_held), here))
    ]
    for load in smalls:
        load.start()
    def strip_held(side, strip):
        column = pl.multiple_of((side * half + strip) * LANES, LANES)
        return tiles.at[0, :, pl.ds(column, LANES)]

    loads = [
        pltpu.make_async_copy(strip_held(core, strip), own.at[strip], load_sem.at[strip])
        for strip in range(half)
    ]
    loads.append(pltpu.make_async_copy(rings_held, rings, load_sem.at[STRIPS]))
    loads.append(pltpu.make_async_copy(taps_held, taps, load_sem.at[STRIPS + 1]))
    for load in loads[:half]:
        load.start()

    for load in smalls:
        load.wait()
    probe_row = positions[0, probe_id] - row_start
    probe_column = positions[1, probe_id]

    lane = lax.broadcasted_iota(jnp.int32, (1, 1, LANES), 2)
    payload = jnp.zeros((1, 1, LANES), F32)
    for beam in range(2):
        values = (
            tilts[beam, 0].astype(F32),
            tilts[beam, 1].astype(F32),
            amplitude[beam],
            angle[beam],
        )
        for n, value in enumerate(values):
            payload = jnp.where(lane == 4 * beam + n, value, payload)
    beams[pl.ds(me, 1)] = payload

    for beam in range(2):
        tilt_row, tilt_column = tilts[beam, 0], tilts[beam, 1]
        pc, ps = phasor(tilt_row * lax.broadcasted_iota(jnp.int32, (8, BLOCK_IN), 1))
        pc, ps = pc[:1], ps[:1]
        real = taps_real[...] * pc - taps_imag[...] * ps
        imag = taps_real[...] * ps + taps_imag[...] * pc
        low = 2 * BLOCK * beam
        beam_taps[low : low + BLOCK, :] = jnp.concatenate([real, -imag], axis=1).astype(BF16)
        low += BLOCK
        beam_taps[low : low + BLOCK, :] = jnp.concatenate([imag, real], axis=1).astype(BF16)
        starts = row_start - BEFORE + BLOCK * lax.broadcasted_iota(jnp.int32, (8, NPIX), 0)
        pc, ps = phasor(
            tilt_row * starts + tilt_column * lax.broadcasted_iota(jnp.int32, (8, NPIX), 1)
        )
        phase[beam, 0] = pc
        phase[beam, 1] = ps

    pl.semaphore_wait(barrier, len(partners))
    started = []

    def copy_of(source, target, send_at, recv_at, device):
        return pltpu.make_async_remote_copy(
            src_ref=source,
            dst_ref=target,
            send_sem=send_at,
            recv_sem=recv_at,
            device_id=device,
            device_id_type=MESH,
        )

    def send(*args):
        copy = copy_of(*args)
        copy.start()
        started.append(copy)
        return copy

    def beam_chunk(size):
        return beams.at[pl.ds(pl.multiple_of(me // size * size, size), size)]

    chunk = beam_chunk(1)
    beam_copies = [send(chunk, chunk, beam_send.at[0], beam_recv.at[0], (twin, block))]
    swaps = [
        send(
            strip_held(1 - core, strip),
            other.at[strip],
            swap_send.at[strip],
            swap_recv.at[strip],
            (twin, block),
        )
        for strip in range(half)
    ]
    for load in loads[:half]:
        load.wait()
    for load in loads[half:]:
        load.start()

    def beam_step(size, devices, slot):
        for copy in beam_copies:
            copy.wait_recv()
        chunk = beam_chunk(size)
        beam_copies[:] = [
            send(chunk, chunk, beam_send.at[slot + k], beam_recv.at[slot + k], (device, block))
            for k, device in enumerate(devices)
        ]

    for swap in swaps:
        swap.wait_recv()

    copies = [None, None]

    def out_along_first(s):
        keep_own = jnp.where(owners[s] == me, 1.0, 0.0)
        keep_other = jnp.where(owners[s] == twin, 1.0, 0.0)
        for strip in range(half):
            value = own[strip].astype(F32) * keep_own + other[strip].astype(F32) * keep_other
            masked[s, strip] = value.astype(BF16)
        copies[s] = [
            send(
                masked.at[s, (place1 + k + 1) % 4],
                arrived1.at[s, k],
                send_sem.at[s, k],
                recv_sem.at[s, k],
                (line1[k], block),
            )
            for k in range(3)
        ]

    def out_along_second(s):
        for copy in copies[s]:
            copy.wait_recv()
        total = masked[s, place1].astype(F32)
        for k in range(3):
            total += arrived1[s, k].astype(F32)
        summed1[s] = total.astype(BF16)
        copies[s] = [
            send(
                summed1.at[s, pl.ds(pl.multiple_of((place2 + k + 1) % 4 * piece, piece), piece)],
                arrived2.at[s, k],
                send_sem.at[s, k + 3],
                recv_sem.at[s, k + 3],
                (line2[k], block),
            )
            for k in range(3)
        ]

    out_along_first(0)
    beam_step(2, along_x, 1)
    out_along_first(1)
    out_along_second(0)
    beam_step(8, along_y, 4)
    out_along_second(1)

    edge_to = [(me, 1 - block), (facing, 1 - block)]
    edges = [
        (0, pl.ds(0, AFTER), after_in, pl.ds(BEFORE + rows, AFTER)),
        (3, pl.ds(piece - BEFORE, BEFORE), before_in, pl.ds(0, BEFORE)),
    ]

    def edge_copies(s, n):
        _, source, target, _ = edges[n]
        return [
            copy_of(
                summed2.at[s, source],
                target.at[s, k],
                edge_send.at[s, n, k],
                edge_recv.at[s, n, k],
                edge_to[k],
            )
            for k in range(2)
        ]

    def edge_spread(s, n, peers=range(3)):
        place = kept.at[s, strip, edges[n][3]]
        return [
            copy_of(
                place, place, edge_send.at[s, n, k + 2], edge_recv.at[s, n, 2], (line2[k], block)
            )
            for k in peers
        ]

    mine = pl.ds(pl.multiple_of(place2 * piece, piece), piece)
    mine_kept = pl.ds(pl.multiple_of(place2 * piece + BEFORE, BEFORE), piece)
    strip = core * half + place1

    def out_to_facing(s):
        for copy in copies[s]:
            copy.wait_recv()
        total = summed1[s, mine].astype(F32)
        for k in range(3):
            total += arrived2[s, k].astype(F32)
        summed2[s] = total.astype(BF16)
        copies[s] = [
            send(
                summed2.at[s],
                arrived3.at[s],
                send_sem.at[s, 6],
                recv_sem.at[s, 6],
                (facing, block),
            )
        ]
        for n in range(2):

            @pl.when(place2 == edges[n][0])
            def _(n=n):
                for copy in edge_copies(s, n):
                    copy.start()

    def back_along_second(s):
        copies[s][0].wait_recv()
        kept[s, strip, mine_kept] = (
            summed2[s].astype(F32) + arrived3[s].astype(F32)
        ).astype(BF16)
        place = kept.at[s, strip, mine_kept]
        copies[s] = [
            send(place, place, send_sem.at[s, k + 7], recv_sem.at[s, k + 7], (line2[k], block))
            for k in range(3)
        ]
        for n in range(2):

            @pl.when(place2 == edges[n][0])
            def _(n=n):
                for copy in edge_copies(s, n):
                    copy.wait_recv()
                arrived = edges[n][2]
                total = arrived[s, 0].astype(F32) + arrived[s, 1].astype(F32)
                kept[s, strip, edges[n][3]] = total.astype(BF16)
                for copy in edge_spread(s, n):
                    copy.start()

        onward(s, mine_kept)

    def line_copy(s, k, held, at_strip):
        place = kept.at[s, at_strip, held]
        return copy_of(
            place, place, send_sem.at[s, k + 10], recv_sem.at[s, k + 10], (line1[k], block)
        )

    def onward(s, held):
        for k in range(3):
            line_copy(s, k, held, strip).start()

    def strip_to_twin(s, n, at_strip):
        place = kept.at[s, at_strip]
        twin_copies[s].append(
            send(place, place, twin_send.at[s, n], twin_recv.at[s, n], (twin, block))
        )

    twin_copies = [[], []]
    whole = pl.ds(0, KEPT)

    def back_along_first(s):
        for k in (0, 2, 1):
            copies[s][k].wait_recv()
            came = (place2 + 3 - k) % 4 * piece + BEFORE
            onward(s, pl.ds(pl.multiple_of(came, BEFORE), piece))
        for n in range(2):

            @pl.when(place2 != edges[n][0])
            def _(n=n):
                edge_spread(s, n, [0])[0].wait_recv()

            onward(s, edges[n][3])
        strip_to_twin(s, 3, strip)

    def back_to_twin(s):
        for k in (0, 2, 1):
            line_copy(s, k, whole, strip).wait_recv()
            strip_to_twin(s, k, core * half + (place1 + 3 - k) % 4)

    out_to_facing(0)
    beam_step(32, [facing], 7)
    out_to_facing(1)
    back_along_second(0)
    back_along_second(1)
    back_along_first(0)
    back_along_first(1)

    for copy in beam_copies:
        copy.wait_recv()
    reach = BLOCK_IN - 4 * RAD
    table = beams[...].reshape(beams.shape[0], LANES)
    both = jnp.concatenate([table[:, 0:4], table[:, 4:8]], axis=0)
    count = both.shape[0]
    ids = lax.broadcasted_iota(jnp.int32, (count, 1), 0)
    ids = jnp.where(ids < count // 2, 2 * ids, 2 * ids - count + 1)
    ky = both[:, 0:1].astype(jnp.int32)
    kx = both[:, 1:2].astype(jnp.int32)
    inside = (((ids - offsets[probe_id] + count) & (count - 1)) < count // 2).astype(F32)
    weight = both[:, 2:3] * inside * (1.0 / math.sqrt(count // 2))
    angle_c, angle_s = circle(both[:, 3:4] * (0.5 / math.pi))
    rel = lax.broadcasted_iota(jnp.int32, (count, LANES), 1) - BEFORE
    pc, ps = phasor(ky * rel - kx * probe_column)
    left_real = weight * (angle_c * pc - angle_s * ps)
    left_imag = weight * (angle_s * pc + angle_c * ps)
    left_real, left_imag = left_real.T[:reach], left_imag.T[:reach]
    left = jnp.concatenate(
        [
            jnp.concatenate([left_real, -left_imag], axis=1),
            jnp.concatenate([left_imag, left_real], axis=1),
        ],
        axis=0,
    )
    high = left.astype(BF16)
    left = jnp.concatenate([high, (left - high.astype(F32)).astype(BF16)], axis=0)
    pc, ps = phasor(kx * lax.broadcasted_iota(jnp.int32, (count, LANES), 1))
    qc, qs = phasor(kx * (LANES * lax.broadcasted_iota(jnp.int32, (count, STRIPS), 1)))
    for pair in range(STRIPS // 2):
        right = []
        for n in (2 * pair, 2 * pair + 1):
            c, s = qc[:, n : n + 1], qs[:, n : n + 1]
            right.append(jnp.concatenate([pc * c - ps * s, pc * s + ps * c], axis=0).astype(BF16))
        wave = dot(left, jnp.concatenate(right, axis=1))
        columns = slice(pair * 2 * LANES, (pair + 1) * 2 * LANES)
        incident[:, columns] = wave[: 2 * reach] + wave[2 * reach :]

    back_to_twin(0)

    def window(s, first, count, pair):
        chosen = lax.broadcasted_iota(jnp.int32, (count, KEPT), 0) + first
        chosen = (lax.broadcasted_iota(jnp.int32, (count, KEPT), 1) == chosen).astype(BF16)
        held = jnp.concatenate([kept[s, 2 * pair], kept[s, 2 * pair + 1]], axis=1)
        c, s = cos_sin(dot(chosen, held))
        return c.astype(BF16).astype(F32), s.astype(BF16).astype(F32)

    def factors0(side):
        def factors(step, carry):
            held = pl.ds(pl.multiple_of(step * STEP, 16), STEP)
            for n in range(half):
                at_strip = side * half + n
                columns = pl.ds(pl.multiple_of(at_strip * LANES, LANES), LANES)
                c, s = cos_sin(kept[0, at_strip, held, :].astype(F32))
                factor0[0, held, columns] = c.astype(BF16)
                factor0[1, held, columns] = s.astype(BF16)
            return carry

        lax.fori_loop(0, factor0.shape[1] // STEP, factors, 0)

    def probe_in(side):
        for n in range(half // 2):
            pair = side * (half // 2) + n
            columns = pl.ds(pl.multiple_of(pair * 2 * LANES, 2 * LANES), 2 * LANES)
            fr, fi = window(0, probe_row, reach, pair)
            r, i = incident[:reach, columns], incident[reach:, columns]
            field[:reach, columns] = (r * fr - i * fi).astype(BF16)
            field[BLOCK_IN : BLOCK_IN + reach, columns] = (r * fi + i * fr).astype(BF16)

    field[...] = jnp.zeros(field.shape, BF16)
    factors0(core)
    probe_in(core)
    for copy in twin_copies[0]:
        copy.wait_recv()
    factors0(1 - core)
    back_to_twin(1)

    def factors1(side):
        def factors(step, carry):
            start = pl.multiple_of(step * STEP, 16)
            for n in range(half):
                at_strip = side * half + n
                columns = pl.ds(pl.multiple_of(at_strip * LANES, LANES), LANES)
                values = kept[1, at_strip, pl.ds(start, STEP + 16), :].astype(F32)
                c, s = cos_sin(values[RAD : RAD + STEP])
                factor1[0, pl.ds(start, STEP), columns] = c.astype(BF16)
                factor1[1, pl.ds(start, STEP), columns] = s.astype(BF16)
            return carry

        lax.fori_loop(0, factor1.shape[1] // STEP, factors, 0)

    factors1(core)
    probe_in(1 - core)
    for copy in twin_copies[1]:
        copy.wait_recv()
    factors1(1 - core)
    for load in loads[half:]:
        load.wait()

    def turned(mixed, count, beam, block):
        real, imag = mixed[:count], mixed[count:]
        pc = phase[beam, 0, pl.ds(block, 1), :]
        ps = phase[beam, 1, pl.ds(block, 1), :]
        return split(real * pc - imag * ps, real * ps + imag * pc)

    def pass_on(quarters, start, count):
        for q, (real, imag) in enumerate(quarters):
            columns = slice(q * QUARTER, (q + 1) * QUARTER)
            fr = factor1[0, pl.ds(start, count), columns].astype(F32)
            fi = factor1[1, pl.ds(start, count), columns].astype(F32)
            for beam in range(2):
                r, i = real[beam * count : (beam + 1) * count], imag[beam * count : (beam + 1) * count]
                passed[beam, 0, pl.ds(start, count), columns] = (r * fr - i * fi).astype(BF16)
                passed[beam, 1, pl.ds(start, count), columns] = (r * fi + i * fr).astype(BF16)

    def store(n, start, count):
        part = pl.ds(start, count)
        return pltpu.make_async_copy(
            passed.at[:, :, part], passed_out.at[:, :, part], store_sem.at[n]
        )

    def block_of(start):
        return jnp.concatenate(
            [factor0[0, pl.ds(start, BLOCK_IN), :], factor0[1, pl.ds(start, BLOCK_IN), :]], axis=0
        )

    def first_block(block, carry):
        start = pl.multiple_of(block * BLOCK, 16)
        mixed = dot(beam_taps[...], block_of(start))
        parts = [
            turned(mixed[2 * BLOCK * beam : 2 * BLOCK * (beam + 1)], BLOCK, beam, block)
            for beam in range(2)
        ]
        pass_on(propagate(parts, rings), start, BLOCK)
        store(block, start, BLOCK).start()
        return carry

    lax.fori_loop(0, FULL_BLOCKS, first_block, 0, unroll=2)

    out = PASSED - TAIL
    tops = [BLOCK * n for n in range(4)]
    left = jnp.concatenate([beam_taps[top : top + out] for top in tops])
    mixed = dot(left, block_of(TAIL))
    parts = [
        turned(mixed[2 * out * beam : 2 * out * (beam + 1)], out, beam, FULL_BLOCKS)
        for beam in range(2)
    ]
    mixed = dot(jnp.concatenate([taps[:out], taps[BLOCK : BLOCK + out]]), field[...])
    parts.append(split(mixed[:out], mixed[out:]))
    quarters = propagate(parts, rings)
    pass_on(quarters, TAIL, out)
    last = store(FULL_BLOCKS, TAIL, out)
    last.start()
    field[...] = jnp.zeros(field.shape, BF16)
    for pair in range(STRIPS // 2):
        columns = slice(pair * 2 * LANES, (pair + 1) * 2 * LANES)
        r, i = [
            jnp.concatenate([quarters[2 * pair + n][part][2 * out :] for n in range(2)], axis=1)
            for part in range(2)
        ]
        fr, fi = window(1, probe_row + RAD, out, pair)
        field[:out, columns] = (r * fr - i * fi).astype(BF16)
        field[BLOCK_IN : BLOCK_IN + out, columns] = (r * fi + i * fr).astype(BF16)
    field_copy = pltpu.make_async_copy(field, field_out, store_sem.at[FULL_BLOCKS + 1])
    field_copy.start()

    for copy in started:
        copy.wait_send()
    for s in range(2):
        for k in range(3):
            line_copy(s, k, whole, strip).wait_send()
        for n in range(2):

            @pl.when(place2 == edges[n][0])
            def _(s=s, n=n):
                for copy in edge_copies(s, n) + edge_spread(s, n):
                    copy.wait_send()

    for n in range(FULL_BLOCKS):
        store(n, n * BLOCK, BLOCK).wait()
    last.wait()
    field_copy.wait()


def first_slice(owners, tilts, amplitude, angle, positions, offsets, tiles):
    real, imag = row_matrices()
    taps = np.block([[real, -imag], [imag, real]]).astype(ml_dtypes.bfloat16)
    half = STRIPS // 2
    rows = tiles.shape[1]
    piece = rows // 4
    anywhere = pl.BlockSpec(memory_space=pl.ANY)
    reach = BLOCK_IN - 4 * RAD
    return pl.pallas_call(
        first_kernel,
        out_shape=(
            jax.ShapeDtypeStruct((2, 2, PASSED, NPIX), BF16),
            jax.ShapeDtypeStruct((2 * BLOCK_IN, NPIX), BF16),
        ),
        in_specs=[anywhere] * 11,
        out_specs=(anywhere, anywhere),
        scratch_shapes=[
            pltpu.SMEM(owners.shape, owners.dtype),
            pltpu.SMEM(tilts.shape, tilts.dtype),
            pltpu.SMEM(amplitude.shape, amplitude.dtype),
            pltpu.SMEM(angle.shape, angle.dtype),
            pltpu.SMEM(positions.shape, positions.dtype),
            pltpu.SMEM(offsets.shape, offsets.dtype),
            pltpu.VMEM(real.shape, F32),
            pltpu.VMEM(real.shape, F32),
            pltpu.VMEM((lax.axis_size("beam"), 1, LANES), F32),
            pltpu.VMEM((half, rows, LANES), BF16),
            pltpu.VMEM((half, rows, LANES), BF16),
            pltpu.VMEM((2, half, rows, LANES), BF16),
            pltpu.VMEM((2, 3, rows, LANES), BF16),
            pltpu.VMEM((2, rows, LANES), BF16),
            pltpu.VMEM((2, 3, piece, LANES), BF16),
            pltpu.VMEM((2, piece, LANES), BF16),
            pltpu.VMEM((2, piece, LANES), BF16),
            pltpu.VMEM((2, 2, AFTER, LANES), BF16),
            pltpu.VMEM((2, 2, BEFORE, LANES), BF16),
            pltpu.VMEM((2, STRIPS, KEPT, LANES), BF16),
            pltpu.VMEM((2 * BLOCK, 2 * BLOCK_IN), BF16),
            pltpu.VMEM((RINGS, 2 * QUARTER, 2 * QUARTER), BF16),
            pltpu.VMEM((2, TAIL + BLOCK_IN, NPIX), BF16),
            pltpu.VMEM((2, PASSED, NPIX), BF16),
            pltpu.VMEM((4 * BLOCK, 2 * BLOCK_IN), BF16),
            pltpu.VMEM((2, 2, 8, NPIX), F32),
            pltpu.VMEM((2 * reach, NPIX), F32),
            pltpu.VMEM((2 * BLOCK_IN, NPIX), BF16),
            pltpu.VMEM((2, 2, PASSED, NPIX), BF16),
            pltpu.SemaphoreType.DMA((STRIPS + 10,)),
            pltpu.SemaphoreType.DMA((half,)),
            pltpu.SemaphoreType.DMA((half,)),
            pltpu.SemaphoreType.DMA((2, 13)),
            pltpu.SemaphoreType.DMA((2, 13)),
            pltpu.SemaphoreType.DMA((2, 4)),
            pltpu.SemaphoreType.DMA((2, 4)),
            pltpu.SemaphoreType.DMA((2, 2, 5)),
            pltpu.SemaphoreType.DMA((2, 2, 3)),
            pltpu.SemaphoreType.DMA((8,)),
            pltpu.SemaphoreType.DMA((8,)),
            pltpu.SemaphoreType.DMA((FULL_BLOCKS + 2,)),
        ],
        compiler_params=pltpu.CompilerParams(
            collective_id=0, has_side_effects=True, vmem_limit_bytes=60 * 2**20
        ),
        name="first_slice",
    )(
        owners,
        tilts,
        amplitude,
        angle,
        positions,
        offsets,
        tiles,
        jnp.asarray(real),
        jnp.asarray(imag),
        jnp.asarray(taps),
        jnp.asarray(ring_matrices()),
    )


def second_kernel(
    positions_held,
    taps_held,
    rings_held,
    passed_in,
    field_in,
    exit_out,
    probe,
    positions,
    taps,
    rings,
    field,
    passed,
    waves,
    load_sem,
    store_sem,
):
    probe_id = lax.axis_index("row") * lax.axis_size("beam") + lax.axis_index("beam")
    pairs = (
        (taps_held, taps),
        (rings_held, rings),
        (field_in, field),
        (positions_held, positions),
    )
    loads, others = [], []
    end = 0
    for n in range(FULL_BLOCKS + 1):
        start, end = end, min(n * BLOCK + BLOCK_IN, PASSED)
        loads.append(
            pltpu.make_async_copy(
                passed_in.at[:, :, start:end], passed.at[:, :, start:end], load_sem.at[n]
            )
        )
        loads[n].start()
        if n == 0:
            for m, pair in enumerate(pairs):
                others.append(pltpu.make_async_copy(*pair, load_sem.at[FULL_BLOCKS + 1 + m]))
                others[m].start()
    spare = passed.shape[2] - PASSED
    passed[:, :, PASSED:, :] = jnp.zeros((2, 2, spare, NPIX), BF16)

    def block_of(beam, start):
        return jnp.concatenate(
            [passed[beam, 0, start : start + BLOCK_IN], passed[beam, 1, start : start + BLOCK_IN]],
            axis=0,
        )

    stores = []

    def write(quarters, start, count):
        for q, (real, imag) in enumerate(quarters):
            for beam in range(2):
                chosen = slice(beam * count, (beam + 1) * count)
                low = q * QUARTER
                waves[beam, start : start + count, low : low + QUARTER] = real[chosen].astype(BF16)
                low += NPIX
                waves[beam, start : start + count, low : low + QUARTER] = imag[chosen].astype(BF16)
        part = slice(start, start + count)
        stores.append(
            pltpu.make_async_copy(
                waves.at[:, part], exit_out.at[:, part], store_sem.at[len(stores)]
            )
        )
        stores[-1].start()

    others[0].wait()
    for block in range(FULL_BLOCKS):
        loads[block].wait()
        start = block * BLOCK
        parts = []
        for beam in range(2):
            mixed = dot(taps[...], block_of(beam, start))
            parts.append(split(mixed[:BLOCK], mixed[BLOCK:]))
        if block == 0:
            others[1].wait()
        write(propagate(parts, rings), start, BLOCK)

    loads[FULL_BLOCKS].wait()
    others[2].wait()
    others[3].wait()
    left = jnp.concatenate([taps[:WIN], taps[BLOCK : BLOCK + WIN]])
    parts = []
    for mixed in [dot(left, block_of(beam, TAIL)) for beam in range(2)] + [dot(left, field[...])]:
        parts.append(split(mixed[:WIN], mixed[WIN:]))
    quarters = propagate(parts, rings)
    write(quarters, TAIL, WIN)
    shift = (NPIX - positions[1, probe_id]) & (NPIX - 1)
    real = jnp.concatenate([real[2 * WIN :] for real, _ in quarters], axis=1)
    imag = jnp.concatenate([imag[2 * WIN :] for _, imag in quarters], axis=1)
    real = pltpu.roll(real, shift, 1)[:, :WIN]
    imag = pltpu.roll(imag, shift, 1)[:, :WIN]
    probe[0, 0] = jnp.concatenate([real, imag], axis=1)
    for copy in stores:
        copy.wait()


def second_slice(positions, passed, field):
    real, imag = row_matrices()
    taps = np.block([[real, -imag], [imag, real]]).astype(ml_dtypes.bfloat16)
    vmem = pl.BlockSpec(memory_space=pltpu.VMEM)
    anywhere = pl.BlockSpec(memory_space=pl.ANY)
    return pl.pallas_call(
        second_kernel,
        out_shape=(
            jax.ShapeDtypeStruct((2, NPIX // 2, 2 * NPIX), BF16),
            jax.ShapeDtypeStruct((1, 1, WIN, 2 * WIN), F32),
        ),
        in_specs=[anywhere] * 5,
        out_specs=(anywhere, vmem),
        scratch_shapes=[
            pltpu.SMEM(positions.shape, positions.dtype),
            pltpu.VMEM((2 * BLOCK, 2 * BLOCK_IN), BF16),
            pltpu.VMEM((RINGS, 2 * QUARTER, 2 * QUARTER), BF16),
            pltpu.VMEM((2 * BLOCK_IN, NPIX), BF16),
            pltpu.VMEM((2, 2, TAIL + BLOCK_IN, NPIX), BF16),
            pltpu.VMEM((2, NPIX // 2, 2 * NPIX), BF16),
            pltpu.SemaphoreType.DMA((FULL_BLOCKS + 5,)),
            pltpu.SemaphoreType.DMA((FULL_BLOCKS + 1,)),
        ],
        compiler_params=pltpu.CompilerParams(vmem_limit_bytes=60 * 2**20),
        name="second_slice",
    )(positions, jnp.asarray(taps), jnp.asarray(ring_matrices()), passed, field)


def body(tilts, potentials, owners, beam_amplitude, beam_phase, probe_positions, beam_offsets):
    positions = probe_positions.T
    passed, field = first_slice(
        owners, tilts, beam_amplitude, beam_phase, positions, beam_offsets, potentials
    )
    return second_slice(positions, passed, field)


def solution(mesh):
    return jax.shard_map(
        body,
        mesh=mesh,
        in_specs=(P("beam", None), P("beam", "row", None), P(), P("beam"), P("beam"), P(), P()),
        out_specs=(P("beam", "row", None), P("row", "beam", None, None)),
        check_vma=False,
    )
```
